32 devices in a mesh: dp: 8 (over y, x, core), tensor: 4 (over z).
Axes of the slice: x: 2, y: 2, z: 4, core: 2. Of those that a mesh axis runs over, the one named last changes fastest.
Arguments:
- inputs: bfloat16 [4096, 1024], P(('dp', 'tensor')), may hold values from -6 to 6
- segment_ids: int32 [4096], P('dp'), may hold values from -1 to 31, as said below
- ln1_gain: float32 [1024], replicated, may hold values from 0.5 to 1.5
- ln1_bias: float32 [1024], replicated, may hold values from -1.75 to 1.75
- ln2_gain: float32 [1024], replicated, may hold values from 0.5 to 1.5
- ln2_bias: float32 [1024], replicated, may hold values from -1.75 to 1.75
- qkv_weight: bfloat16 [1024, 3072], P('dp', 'tensor'), may hold values from -0.1875 to 0.1875
- qkv_bias: float32 [3072], P('tensor'), may hold values from -1.75 to 1.75
- dense_weight: bfloat16 [1024, 1024], P('dp', 'tensor'), may hold values from -0.5 to 0.5
- dense_bias: float32 [1024], replicated, may hold values from -1.75 to 1.75
- fc1_weight: bfloat16 [1024, 4096], P('dp', 'tensor'), may hold values from -0.1875 to 0.1875
- fc1_bias: float32 [4096], P('tensor'), may hold values from -1.75 to 1.75
- fc2_weight: bfloat16 [1024, 4096], P('dp', 'tensor'), may hold values from -0.09375 to 0.09375
- fc2_bias: float32 [1024], replicated, may hold values from -1.75 to 1.75
- cotangent: bfloat16 [4096, 1024], P(('dp', 'tensor')), may hold values from -6 to 6
Outputs:
- output: bfloat16 [4096, 1024], P(('dp', 'tensor'))
- input_grad: float32 [4096, 1024], P(('dp', 'tensor'))
- ln1_gain_grad: float32 [1024], replicated
- ln1_bias_grad: float32 [1024], replicated
- ln2_gain_grad: float32 [1024], replicated
- ln2_bias_grad: float32 [1024], replicated
- qkv_weight_grad: float32 [1024, 3072], P('dp', 'tensor')
- qkv_bias_grad: float32 [3072], P('tensor')
- dense_weight_grad: float32 [1024, 1024], P('dp', 'tensor')
- dense_bias_grad: float32 [1024], replicated
- fc1_weight_grad: float32 [1024, 4096], P('dp', 'tensor')
- fc1_bias_grad: float32 [4096], P('tensor')
- fc2_weight_grad: float32 [1024, 4096], P('dp', 'tensor')
- fc2_bias_grad: float32 [1024], replicated
The draws below stay inside these ranges and needn't reach their ends.
Inputs may be any that keep to these rules, and one draw needn't show every extreme that they name: `segment_ids`: in each group of 512 rows the tokens with id >= 0 come first, 128 times a whole number of them (at least one block); their ids start at 0 and never fall, and a new sequence starts only at a multiple of 16 slots. Padding has id -1. In every draw some group has no padding and starts a sequence at every such multiple.
All inputs are finite; a program needn't handle non-finite values.
Results may differ from the reference program's by a relative error of at most 0.01.
Values may be sent and summed in bfloat16 or wider, within the bound.
No kernel may reach another device: no remote copies, remote signals or barrier semaphores. Data moves between devices by JAX's collectives and lax.ppermute only.
A program may use at most 128 MiB of HBM per device.

```python
from functools import partial
import jax
import jax.numpy as jnp
from jax import lax

D = 1024
HD = 64
ROT = 16
FF = 4096
BUF = 512
BLK = 128
TOKENS = 4096


def draw_segment_ids(key, part):
    groups = TOKENS // BUF
    blocks = BUF // BLK
    step = max(BLK // 8, 1)
    first_key, second_key, third_key = jax.random.split(jax.random.fold_in(key, 7), 3)
    used_blocks = jax.random.randint(first_key, (groups,), 1, blocks + 1)
    full_group = jax.random.randint(second_key, (), 0, groups)
    is_full = jnp.arange(groups) == full_group
    used_blocks = jnp.where(is_full, blocks, used_blocks)
    slot_index = jnp.arange(BUF, dtype=jnp.int32)
    on_grid = slot_index % step == 0
    starts = jax.random.randint(third_key, (groups, BUF), 0, 8) == 0
    starts = (starts | is_full[:, None]) & on_grid[None, :]
    starts = starts | (slot_index[None, :] == 0)
    numbers = jnp.cumsum(starts.astype(jnp.int32), axis=1) - 1
    filled = slot_index[None, :] < (used_blocks * BLK)[:, None]
    return jnp.where(filled, numbers, -1).reshape(groups * BUF).astype(jnp.int32)


def block_scale(key, extent, cuts, low, largest):
    factor_of = 1.0
    for axis_at, parts in cuts:
        steps = jax.random.uniform(jax.random.fold_in(jax.random.fold_in(key, 6), axis_at), (parts,), jnp.float32, low / len(cuts), largest / len(cuts))
        factor_of = factor_of * jnp.repeat(jnp.exp(steps), extent[axis_at] // parts).reshape((-1,) + (1,) * (len(extent) - 1 - axis_at))
    return factor_of


def bell_draw(stream_key, shape, spread, reach, cuts=(), kind=jnp.bfloat16):
    values = jax.random.normal(stream_key, shape, jnp.float32) * spread
    if len(cuts) > 0:
        values = block_scale(stream_key, shape, cuts, -0.22, 0.18) * values
    return jnp.clip(values, min=-reach, max=reach).astype(kind)


def setup_inputs(seed: int = 0) -> dict:
    keys = jax.random.split(jax.random.key(seed), 16)
    inputs = bell_draw(keys[0], (TOKENS, D), 1.0, 6.0, ((0, 32),))
    segment_ids = draw_segment_ids(jax.random.fold_in(keys[15], 71), 0)
    ln1_gain = jnp.clip(1.0 + 0.1 * jax.random.normal(keys[2], (D,), jnp.float32), 0.5, 1.5)
    ln1_bias = bell_draw(keys[3], (D,), 0.3, 1.75, (), jnp.float32)
    ln2_gain = jnp.clip(1.0 + 0.1 * jax.random.normal(keys[4], (D,), jnp.float32), 0.5, 1.5)
    ln2_bias = bell_draw(keys[5], (D,), 0.3, 1.75, (), jnp.float32)
    qkv_weight = bell_draw(keys[6], (D, 3 * D), D ** -0.5, 0.1875, ((0, 8), (1, 4)))
    qkv_bias = bell_draw(keys[7], (3 * D,), 0.3, 1.75, ((0, 4),), jnp.float32)
    dense_weight = bell_draw(keys[8], (D, D), (D // 8) ** -0.5, 0.5, ((0, 8), (1, 4)))
    dense_bias = bell_draw(keys[9], (D,), 0.3, 1.75, (), jnp.float32)
    fc1_weight = bell_draw(keys[10], (D, FF), D ** -0.5, 0.1875, ((0, 8), (1, 4)))
    fc1_bias = bell_draw(keys[11], (FF,), 0.3, 1.75, ((0, 4),), jnp.float32)
    fc2_weight = bell_draw(keys[12], (D, FF), FF ** -0.5, 0.09375, ((0, 8), (1, 4)))
    fc2_bias = bell_draw(keys[13], (D,), 0.3, 1.75, (), jnp.float32)
    cotangent = bell_draw(keys[14], (TOKENS, D), 1.0, 6.0, ((0, 32),))
    return {"inputs": inputs, "segment_ids": segment_ids, "ln1_gain": ln1_gain, "ln1_bias": ln1_bias, "ln2_gain": ln2_gain, "ln2_bias": ln2_bias, "qkv_weight": qkv_weight, "qkv_bias": qkv_bias, "dense_weight": dense_weight, "dense_bias": dense_bias, "fc1_weight": fc1_weight, "fc1_bias": fc1_bias, "fc2_weight": fc2_weight, "fc2_bias": fc2_bias, "cotangent": cotangent}


EPS = 1e-05

def normalize(embedded, gain, shift):
    center = embedded - lax.optimization_barrier(jnp.mean(embedded, axis=-1, keepdims=True))
    inv_std = lax.rsqrt(lax.optimization_barrier(jnp.mean(center * center, axis=-1, keepdims=True)) + EPS)
    scaled = center * inv_std
    return ((scaled * gain + shift).astype(jnp.bfloat16), scaled, inv_std)

def normalize_back(grads, gain, scaled, inv_std):
    grad_scaled = grads * gain
    grad_input = inv_std * (grad_scaled - lax.optimization_barrier(jnp.mean(grad_scaled, axis=-1, keepdims=True)) - scaled * lax.optimization_barrier(jnp.mean(grad_scaled * scaled, axis=-1, keepdims=True)))
    return (grad_input, lax.optimization_barrier(jnp.sum(grads * scaled, axis=0)), lax.optimization_barrier(jnp.sum(grads, axis=0)))

def rotary_tables(segment_ids):
    row_index = jnp.arange(segment_ids.shape[0], dtype=jnp.int32)
    earlier = (segment_ids[None, :] >= 0) & (segment_ids[None, :] < segment_ids[:, None])
    position = (row_index - lax.optimization_barrier(jnp.sum(earlier.astype(jnp.int32), axis=1))).astype(jnp.float32)
    half_rot = ROT // 2
    frequency = 10000.0 ** (-2.0 * jnp.arange(half_rot, dtype=jnp.float32) / ROT)
    angles = position[:, None] * frequency[None, :]
    angles = jnp.concatenate([angles, angles], axis=1)
    return (jnp.cos(angles)[:, None, :], jnp.sin(angles)[:, None, :])

def allowed_mask(segment_ids):
    row_index = jnp.arange(segment_ids.shape[0], dtype=jnp.int32)
    same_segment = (segment_ids[:, None] == segment_ids[None, :]) & (segment_ids[:, None] >= 0)
    same_segment = same_segment & (row_index[None, :] < row_index[:, None])
    return same_segment | (row_index[:, None] == row_index[None, :])

def rotate(heads_in, cos_table, sine_table):
    half_rot = ROT // 2
    rotated_part = heads_in[..., :ROT]
    turned = jnp.concatenate([-rotated_part[..., half_rot:], rotated_part[..., :half_rot]], axis=-1)
    return jnp.concatenate([rotated_part * cos_table + turned * sine_table, heads_in[..., ROT:]], axis=-1)

def rotate_back(grads, cos_table, sine_table):
    half_rot = ROT // 2
    rotated_part = grads[..., :ROT]
    scaled_sin = rotated_part * sine_table
    turned = jnp.concatenate([scaled_sin[..., half_rot:], -scaled_sin[..., :half_rot]], axis=-1)
    return jnp.concatenate([rotated_part * cos_table + turned, grads[..., ROT:]], axis=-1)

def score_block(queries, key_rows, allowed):
    scores = jnp.einsum('qhd,khd->hqk', queries.astype(jnp.float32), key_rows.astype(jnp.float32))
    scores = scores * queries.shape[-1] ** (-0.5)
    return jnp.where(allowed[None, :, :], scores, -jnp.inf)

def attend(queries, key_rows, value_rows, allowed, validity):
    scores = score_block(queries, key_rows, allowed)
    row_max = lax.optimization_barrier(jnp.max(scores, axis=-1, keepdims=True))
    logsum = row_max + jnp.log(lax.optimization_barrier(jnp.sum(jnp.exp(scores - row_max), axis=-1, keepdims=True)))
    soft_weights = jnp.exp(scores - logsum).astype(jnp.bfloat16)
    attended = jnp.einsum('hqk,khd->qhd', soft_weights.astype(jnp.float32), value_rows.astype(jnp.float32))
    return ((attended * validity[:, None, None]).astype(jnp.bfloat16), logsum)

def attend_back(queries, key_rows, value_rows, allowed, logsum, grad_out):
    scores = score_block(queries, key_rows, allowed)
    probs_full = jnp.exp(scores - logsum)
    soft_weights = probs_full.astype(jnp.bfloat16)
    grad_soft = jnp.einsum('qhd,khd->hqk', grad_out.astype(jnp.float32), value_rows.astype(jnp.float32))
    row_inner = lax.optimization_barrier(jnp.sum(probs_full * grad_soft, axis=-1, keepdims=True))
    grad_scores = (probs_full * (grad_soft - row_inner) * queries.shape[-1] ** (-0.5)).astype(jnp.bfloat16)
    grad_query = jnp.einsum('hqk,khd->qhd', grad_scores.astype(jnp.float32), key_rows.astype(jnp.float32))
    grad_key = jnp.einsum('hqk,qhd->khd', grad_scores.astype(jnp.float32), queries.astype(jnp.float32))
    grad_value = jnp.einsum('hqk,qhd->khd', soft_weights.astype(jnp.float32), grad_out.astype(jnp.float32))
    return (grad_query, grad_key, grad_value)

def layer_group(inputs, segment_ids, cotangent, parameters):
    ln1_gain, ln1_bias, ln2_gain, ln2_bias, qkv_weight, qkv_bias, dense_weight, dense_bias, fc1_weight, fc1_bias, fc2_weight, fc2_bias = parameters
    length = inputs.shape[0]
    embedded = inputs.astype(jnp.float32)
    validity = (segment_ids >= 0).astype(jnp.float32)
    allowed = allowed_mask(segment_ids)
    cos_table, sine_table = rotary_tables(segment_ids)
    normed1, scaled1, spread1 = normalize(embedded, ln1_gain, ln1_bias)
    normed2, scaled2, spread2 = normalize(embedded, ln2_gain, ln2_bias)
    projected = jnp.dot(normed1, qkv_weight, preferred_element_type=jnp.float32) + qkv_bias
    projected = projected.reshape(length, -1, 3, HD)
    queries = rotate(projected[:, :, 0], cos_table, sine_table).astype(jnp.bfloat16)
    key_rows = rotate(projected[:, :, 1], cos_table, sine_table).astype(jnp.bfloat16)
    value_rows = projected[:, :, 2].astype(jnp.bfloat16)
    attended, logsum = attend(queries, key_rows, value_rows, allowed, validity)
    attended_flat = attended.reshape(length, -1)
    branch = jnp.dot(attended_flat, dense_weight.T, preferred_element_type=jnp.float32)
    hidden = jnp.dot(normed2, fc1_weight, preferred_element_type=jnp.float32) + fc1_bias
    active = jax.nn.gelu(hidden, approximate=False).astype(jnp.bfloat16)
    branch = branch + jnp.dot(active, fc2_weight.T, preferred_element_type=jnp.float32)
    output = (embedded + branch + dense_bias + fc2_bias).astype(jnp.bfloat16)
    masked = cotangent.astype(jnp.float32) * validity[:, None]
    grad_rows = masked.astype(jnp.bfloat16)
    out_bias = lax.optimization_barrier(jnp.sum(masked, axis=0))
    grad_attended = jnp.dot(grad_rows, dense_weight, preferred_element_type=jnp.float32)
    dense_grad = jnp.dot(grad_rows.T, attended_flat, preferred_element_type=jnp.float32)
    grad_active = jnp.dot(grad_rows, fc2_weight, preferred_element_type=jnp.float32)
    fc2_grad = jnp.dot(grad_rows.T, active, preferred_element_type=jnp.float32)
    grad_hidden = jax.vjp(partial(jax.nn.gelu, approximate=False), hidden)[1](grad_active)[0]
    fc1_bias_grad = lax.optimization_barrier(jnp.sum(grad_hidden, axis=0))
    grad_hidden_b = grad_hidden.astype(jnp.bfloat16)
    fc1_grad = jnp.dot(normed2.T, grad_hidden_b, preferred_element_type=jnp.float32)
    grad_normed2 = jnp.dot(grad_hidden_b, fc1_weight.T, preferred_element_type=jnp.float32)
    grad_out = (grad_attended * validity[:, None]).astype(jnp.bfloat16).reshape(length, -1, HD)
    grad_query, grad_key, grad_value = attend_back(queries, key_rows, value_rows, allowed, logsum, grad_out)
    grad_projected = jnp.stack([rotate_back(grad_query, cos_table, sine_table), rotate_back(grad_key, cos_table, sine_table), grad_value], axis=2)
    grad_projected = grad_projected.reshape(length, -1)
    qkv_bias_grad = lax.optimization_barrier(jnp.sum(grad_projected, axis=0))
    grad_projected_b = grad_projected.astype(jnp.bfloat16)
    qkv_grad = jnp.dot(normed1.T, grad_projected_b, preferred_element_type=jnp.float32)
    grad_normed1 = jnp.dot(grad_projected_b, qkv_weight.T, preferred_element_type=jnp.float32)
    back1, gain1, shift1 = normalize_back(grad_normed1, ln1_gain, scaled1, spread1)
    back2, gain2, shift2 = normalize_back(grad_normed2, ln2_gain, scaled2, spread2)
    input_grad = masked + back1 + back2
    grads = (gain1, shift1, gain2, shift2, qkv_grad, qkv_bias_grad, dense_grad, out_bias, fc1_grad, fc1_bias_grad, fc2_grad, out_bias)
    return (output, input_grad, grads)

def add_pair(first, second):
    return first + second

def reference(inputs, segment_ids, ln1_gain, ln1_bias, ln2_gain, ln2_bias, qkv_weight, qkv_bias, dense_weight, dense_bias, fc1_weight, fc1_bias, fc2_weight, fc2_bias, cotangent):
    groups = inputs.shape[0] // BUF
    parameters = (ln1_gain, ln1_bias, ln2_gain, ln2_bias, qkv_weight, qkv_bias, dense_weight, dense_bias, fc1_weight, fc1_bias, fc2_weight, fc2_bias)

    def group_step(totals, group_item):
        output, input_grad, grads = layer_group(group_item[0], group_item[1], group_item[2], parameters)
        return (jax.tree.map(add_pair, totals, grads), (output, input_grad))
    zero_grads = tuple((jnp.zeros(entry.shape, jnp.float32) for entry in parameters))
    totals, (outputs, input_grads) = lax.scan(group_step, zero_grads, (inputs.reshape(groups, BUF, -1), segment_ids.reshape(groups, BUF), cotangent.reshape(groups, BUF, -1)))
    return (outputs.reshape(-1, D), input_grads.reshape(-1, D), totals[0], totals[1], totals[2], totals[3], totals[4], totals[5], totals[6], totals[7], totals[8], totals[9], totals[10], totals[11])
```

```python
from functools import partial

import jax
import jax.numpy as jnp
from jax import lax
from jax.sharding import PartitionSpec as P

HD = 64
ROT = 16
EPS = 1e-05
BF = jnp.bfloat16
F32 = jnp.float32


def dot(a, b):
    return jnp.dot(a, b, preferred_element_type=F32)


def rotary_tables(segment_ids, row_index):
    earlier = (segment_ids[None, :] >= 0) & (segment_ids[None, :] < segment_ids[:, None])
    position = (row_index - jnp.sum(earlier.astype(jnp.int32), axis=1)).astype(F32)
    half_rot = ROT // 2
    frequency = 10000.0 ** (-2.0 * jnp.arange(half_rot, dtype=F32) / ROT)
    angles = position[:, None] * frequency[None, :]
    angles = jnp.concatenate([angles, angles], axis=1)
    return (jnp.cos(angles)[:, None, :], jnp.sin(angles)[:, None, :])


def allowed_mask(segment_ids, row_index):
    same_segment = (segment_ids[:, None] == segment_ids[None, :]) & (segment_ids[:, None] >= 0)
    same_segment = same_segment & (row_index[None, :] < row_index[:, None])
    return same_segment | (row_index[:, None] == row_index[None, :])


def rotate(heads_in, cos_table, sine_table):
    half_rot = ROT // 2
    rotated_part = heads_in[..., :ROT]
    turned = jnp.concatenate([-rotated_part[..., half_rot:], rotated_part[..., :half_rot]], axis=-1)
    return jnp.concatenate(
        [rotated_part * cos_table + turned * sine_table, heads_in[..., ROT:]], axis=-1
    )


def rotate_back(grads, cos_table, sine_table):
    half_rot = ROT // 2
    rotated_part = grads[..., :ROT]
    scaled_sin = rotated_part * sine_table
    turned = jnp.concatenate([scaled_sin[..., half_rot:], -scaled_sin[..., :half_rot]], axis=-1)
    return jnp.concatenate([rotated_part * cos_table + turned, grads[..., ROT:]], axis=-1)


def score_block(queries, key_rows, allowed):
    scores = jnp.einsum("qhd,khd->hqk", queries, key_rows, preferred_element_type=F32)
    scores = scores * queries.shape[-1] ** (-0.5)
    return jnp.where(allowed[None, :, :], scores, -jnp.inf)


def attend(queries, key_rows, value_rows, allowed, validity):
    scores = score_block(queries, key_rows, allowed)
    row_max = jnp.max(scores, axis=-1, keepdims=True)
    logsum = row_max + jnp.log(jnp.sum(jnp.exp(scores - row_max), axis=-1, keepdims=True))
    soft_weights = jnp.exp(scores - logsum).astype(BF)
    attended = jnp.einsum("hqk,khd->qhd", soft_weights, value_rows, preferred_element_type=F32)
    return ((attended * validity[:, None, None]).astype(BF), logsum)


def attend_back(queries, key_rows, value_rows, allowed, logsum, grad_out):
    scores = score_block(queries, key_rows, allowed)
    probs_full = jnp.exp(scores - logsum)
    soft_weights = probs_full.astype(BF)
    grad_soft = jnp.einsum("qhd,khd->hqk", grad_out, value_rows, preferred_element_type=F32)
    row_inner = jnp.sum(probs_full * grad_soft, axis=-1, keepdims=True)
    grad_scores = (probs_full * (grad_soft - row_inner) * queries.shape[-1] ** (-0.5)).astype(BF)
    grad_query = jnp.einsum("hqk,khd->qhd", grad_scores, key_rows, preferred_element_type=F32)
    grad_key = jnp.einsum("hqk,qhd->khd", grad_scores, queries, preferred_element_type=F32)
    grad_value = jnp.einsum("hqk,qhd->khd", soft_weights, grad_out, preferred_element_type=F32)
    return (grad_query, grad_key, grad_value)


def xor_pairs(size, flip):
    return [(i, i ^ flip) for i in range(size)]


def on_device(
    dp,
    tz,
    inputs,
    segment_ids,
    ln1_gain,
    ln1_bias,
    ln2_gain,
    ln2_bias,
    qkv_weight,
    qkv_bias,
    dense_weight,
    dense_bias,
    fc1_weight,
    fc1_bias,
    fc2_weight,
    fc2_bias,
    cotangent,
):
    rows, width = inputs.shape
    length = segment_ids.shape[0]
    chips = dp // 2
    here = lax.axis_index("dp")
    core = here % 2
    chip = here // 2
    tensor = lax.axis_index("tensor")
    step = width // chips

    def turn(values):
        parts = [
            lax.dynamic_slice_in_dim(values, (chip ^ r) * step, step, axis=values.ndim - 1)
            for r in range(chips)
        ]
        return jnp.concatenate(parts, axis=-1)

    def sibling(values):
        return lax.ppermute(values, "dp", xor_pairs(dp, 1))

    def over_chip(values, flip):
        return lax.ppermute(values, "dp", xor_pairs(dp, 2 * flip))

    def over_tensor(values, flip):
        return lax.ppermute(values, "tensor", xor_pairs(tz, flip))

    def gather_chips(block):
        if chips == 4:
            along_x, along_y = over_chip(block, 1), over_chip(block, 2)
            half = block.shape[0] // 2
            far = [over_chip(along_x[:half], 2), over_chip(along_y[half:], 1)]
            return jnp.concatenate([block, along_x, along_y] + far, axis=0)
        blocks = [block]
        flip = 1
        while flip < chips:
            blocks = blocks + [over_chip(one, flip) for one in blocks]
            flip *= 2
        return jnp.concatenate(blocks, axis=0)

    def scatter_chips(whole):
        size = whole.shape[0] // chips
        own = whole[:size]
        blocks = [own] + [whole[size * r : size * (r + 1)].astype(BF) for r in range(1, chips)]
        if chips == 4:
            half = size // 2
            from_x = over_chip(blocks[3][:half], 1)
            from_y = over_chip(blocks[3][half:], 2)
            to_y = jnp.concatenate(
                [(whole[2 * size : 2 * size + half] + from_x).astype(BF), blocks[2][half:]], axis=0
            )
            to_x = jnp.concatenate(
                [blocks[1][:half], (whole[size + half : 2 * size] + from_y).astype(BF)], axis=0
            )
            return own + over_chip(to_x, 1) + over_chip(to_y, 2)
        blocks = [whole[size * r : size * (r + 1)] for r in range(chips)]
        flip = chips // 2
        while flip:
            blocks = [
                blocks[r] + over_chip(blocks[r + flip].astype(BF), flip) for r in range(flip)
            ]
            flip //= 2
        return blocks[0]

    def scatter_rows(partial_sum):
        halves = partial_sum.reshape(2, length, width)
        group = halves[0] + sibling(halves[1].astype(BF))
        shards = group.reshape(tz, rows, width)
        total = shards[0]
        for r in range(1, tz):
            total = total + over_tensor(shards[r].astype(BF), r)
        return total

    def gather_rows(own):
        group = jnp.concatenate([own] + [over_tensor(own, r) for r in range(1, tz)], axis=0)
        return jnp.concatenate([group, sibling(group)], axis=0)

    def half_columns(weight):
        return weight.reshape(weight.shape[0], 2, -1)

    weights = (qkv_weight, fc1_weight, dense_weight, fc2_weight)
    kept = [lax.dynamic_index_in_dim(half_columns(w), core, 1, False) for w in weights]
    given = [lax.dynamic_index_in_dim(half_columns(w), 1 - core, 1, False) for w in weights]

    def both_cores(own, other):
        return jnp.where(core == 0, jnp.stack([own, other]), jnp.stack([other, own])).reshape(
            -1, own.shape[-1]
        )

    pairs = [both_cores(own, sibling(out)) for own, out in zip(kept, given)]
    qkv_full, fc1_full, dense_full, fc2_full = [gather_chips(pair) for pair in pairs]

    own_rows = turn(inputs)
    whole = gather_rows(own_rows).astype(F32)
    own_validity = (segment_ids >= 0).astype(F32)
    own_validity = lax.dynamic_slice_in_dim(own_validity, tensor * rows, rows)
    masked = turn(cotangent).astype(F32) * own_validity[:, None]
    grad_whole = gather_rows(masked.astype(BF))

    segments = jnp.concatenate(
        [lax.dynamic_slice_in_dim(segment_ids, (tensor ^ r) * rows, rows) for r in range(tz)]
    )
    row_index = jnp.concatenate(
        [(tensor ^ r) * rows + jnp.arange(rows, dtype=jnp.int32) for r in range(tz)]
    )
    groups = [segments, sibling(segments)]
    validity = (jnp.concatenate(groups) >= 0).astype(F32)
    gain1, shift1, gain2, shift2 = turn(jnp.stack([ln1_gain, ln1_bias, ln2_gain, ln2_bias]))

    center = whole - jnp.mean(whole, axis=-1, keepdims=True)
    spread = lax.rsqrt(jnp.mean(center * center, axis=-1, keepdims=True) + EPS)
    scaled = center * spread
    normed1 = (scaled * gain1 + shift1).astype(BF)
    normed2 = (scaled * gain2 + shift2).astype(BF)

    half_qkv, half_fc1 = qkv_bias.shape[0] // 2, fc1_bias.shape[0] // 2
    qkv_shift = lax.dynamic_slice_in_dim(qkv_bias, core * half_qkv, half_qkv)
    fc1_shift = lax.dynamic_slice_in_dim(fc1_bias, core * half_fc1, half_fc1)

    projected = dot(normed1, qkv_full) + qkv_shift
    projected = projected.reshape(2, length, -1, 3, HD)
    tables = [rotary_tables(one, row_index) for one in groups]
    masks = [allowed_mask(one, row_index) for one in groups]
    kept_state = []
    attended = []
    for g in range(2):
        queries = rotate(projected[g, :, :, 0], *tables[g]).astype(BF)
        key_rows = rotate(projected[g, :, :, 1], *tables[g]).astype(BF)
        value_rows = projected[g, :, :, 2].astype(BF)
        one, logsum = attend(
            queries, key_rows, value_rows, masks[g], validity[g * length : (g + 1) * length]
        )
        kept_state.append((queries, key_rows, value_rows, masks[g], logsum))
        attended.append(one.reshape(length, -1))
    attended = jnp.concatenate(attended, axis=0)

    hidden = dot(normed2, fc1_full) + fc1_shift
    active = jax.nn.gelu(hidden, approximate=False).astype(BF)
    branch = dot(attended, dense_full.T) + dot(active, fc2_full.T)
    summed = scatter_rows(branch)
    output = inputs.astype(F32) + turn(summed) + dense_bias + fc2_bias

    grad_attended = dot(grad_whole, dense_full)
    grad_active = dot(grad_whole, fc2_full)
    fc2_grad = scatter_chips(dot(grad_whole.T, active))
    dense_grad = scatter_chips(dot(grad_whole.T, attended))
    grad_hidden = jax.vjp(partial(jax.nn.gelu, approximate=False), hidden)[1](grad_active)[0]
    fc1_bias_part = jnp.sum(grad_hidden, axis=0)
    grad_hidden_b = grad_hidden.astype(BF)
    fc1_grad = scatter_chips(dot(normed2.T, grad_hidden_b))
    grad_normed2 = dot(grad_hidden_b, fc1_full.T)

    grad_out = (grad_attended * validity[:, None]).astype(BF).reshape(2, length, -1, HD)
    grad_projected = []
    for g in range(2):
        grad_query, grad_key, grad_value = attend_back(*kept_state[g], grad_out[g])
        one = jnp.stack(
            [rotate_back(grad_query, *tables[g]), rotate_back(grad_key, *tables[g]), grad_value],
            axis=2,
        )
        grad_projected.append(one.reshape(length, -1))
    grad_projected = jnp.concatenate(grad_projected, axis=0)
    qkv_bias_part = jnp.sum(grad_projected, axis=0)
    grad_projected_b = grad_projected.astype(BF)
    qkv_grad = scatter_chips(dot(normed1.T, grad_projected_b))
    grad_normed1 = dot(grad_projected_b, qkv_full.T)

    back = scatter_rows(grad_normed1 * gain1 + grad_normed2 * gain2)
    own_scaled, own_spread = scaled[:rows], spread[:rows]
    input_grad = own_spread * (
        back
        - jnp.mean(back, axis=-1, keepdims=True)
        - own_scaled * jnp.mean(back * own_scaled, axis=-1, keepdims=True)
    )
    input_grad = turn(masked + input_grad)

    sums = turn(
        jnp.stack(
            [
                jnp.sum(grad_normed1 * scaled, axis=0),
                jnp.sum(grad_normed1, axis=0),
                jnp.sum(grad_normed2 * scaled, axis=0),
                jnp.sum(grad_normed2, axis=0),
                jnp.sum(masked, axis=0),
            ]
        )
    )
    biases = jnp.zeros((2 * half_qkv + 2 * half_fc1,), F32)
    biases = lax.dynamic_update_slice_in_dim(biases, qkv_bias_part, core * half_qkv, 0)
    biases = lax.dynamic_update_slice_in_dim(
        biases, fc1_bias_part, 2 * half_qkv + core * half_fc1, 0
    )
    flip = 1
    while flip < dp:
        sums = sums + lax.ppermute(sums, "dp", xor_pairs(dp, flip))
        biases = biases + lax.ppermute(biases, "dp", xor_pairs(dp, flip))
        flip *= 2
    flip = 1
    while flip < tz:
        sums = sums + over_tensor(sums, flip)
        flip *= 2

    def to_owner(block):
        size = block.shape[0] // 2
        mine = lax.dynamic_slice_in_dim(block, core * size, size)
        other = sibling(lax.dynamic_slice_in_dim(block, (1 - core) * size, size))
        return jnp.where(
            core == 0, jnp.stack([mine, other], axis=1), jnp.stack([other, mine], axis=1)
        ).reshape(size, -1)

    return (
        output.astype(BF),
        input_grad,
        sums[0],
        sums[1],
        sums[2],
        sums[3],
        to_owner(qkv_grad),
        biases[: 2 * half_qkv],
        to_owner(dense_grad),
        sums[4],
        to_owner(fc1_grad),
        biases[2 * half_qkv :],
        to_owner(fc2_grad),
        sums[4],
    )


def solution(mesh):
    return jax.shard_map(
        partial(on_device, mesh.shape["dp"], mesh.shape["tensor"]),
        mesh=mesh,
        in_specs=(
            P(("dp", "tensor"), None),
            P("dp"),
            P(),
            P(),
            P(),
            P(),
            P("dp", "tensor"),
            P("tensor"),
            P("dp", "tensor"),
            P(),
            P("dp", "tensor"),
            P("tensor"),
            P("dp", "tensor"),
            P(),
            P(("dp", "tensor"), None),
        ),
        out_specs=(
            P(("dp", "tensor"), None),
            P(("dp", "tensor"), None),
            P(),
            P(),
            P(),
            P(),
            P("dp", "tensor"),
            P("tensor"),
            P("dp", "tensor"),
            P(),
            P("dp", "tensor"),
            P("tensor"),
            P("dp", "tensor"),
            P(),
        ),
        check_vma=False,
    )
```

```python
from functools import partial

import jax
import jax.numpy as jnp
from jax import lax
from jax.experimental import pallas as pl
from jax.experimental.pallas import tpu as pltpu
from jax.sharding import PartitionSpec as P

HD = 64
ROT = 16
EPS = 1e-05
BF = jnp.bfloat16
F32 = jnp.float32
CHUNK = 64
ANY = pl.BlockSpec(memory_space=pl.ANY)
VMEM = pl.BlockSpec(memory_space=pltpu.VMEM)
SMEM = pl.BlockSpec(memory_space=pltpu.SMEM)
VMEM_LIMIT = 16 * 1024 * 1024
PEAK = 1.15e9
LITTLE = 0.01


def dot(a, b):
    return jnp.dot(a, b, preferred_element_type=F32)


def dot_nt(a, b):
    return lax.dot_general(a, b, (((1,), (1,)), ((), ())), preferred_element_type=F32)


def dot_tn(a, b):
    return lax.dot_general(a, b, (((0,), (0,)), ((), ())), preferred_element_type=F32)


def shape(dims, dtype):
    return jax.ShapeDtypeStruct(dims, dtype)


def kernel_call(body, name, outs, operands, scratch, micros, fetched=(), placed=False):
    return pl.pallas_call(
        body,
        name=name,
        out_shape=outs,
        in_specs=[SMEM] + [VMEM] * (len(operands) - 1) + [ANY] * len(fetched),
        out_specs=[ANY if placed else VMEM] * len(outs),
        scratch_shapes=scratch,
        cost_estimate=pl.CostEstimate(
            flops=int(micros * PEAK), bytes_accessed=0, transcendentals=0
        ),
        compiler_params=pltpu.CompilerParams(vmem_limit_bytes=VMEM_LIMIT),
    )(*operands, *fetched)


def start_all(pairs, sems, first=0):
    copies = [
        pltpu.make_async_copy(src, dst, sems.at[first + i]) for i, (src, dst) in enumerate(pairs)
    ]
    for one in copies:
        one.start()
    return copies


def wait_all(copies):
    for one in copies:
        one.wait()


def rows_at(start, size):
    return pl.ds(pl.multiple_of(start, size), size)


def shard_rows(place, tz, rows, i):
    return i // tz * tz * rows + (place[1] ^ (i % tz)) * rows


def weight_rows(place, size, i):
    return (i - i % 2 + (place[0] ^ (i % 2))) * size


def rotated(values, cos_table, sine_table):
    lane = lax.broadcasted_iota(jnp.int32, values.shape, 1)
    lanes = values.shape[1]
    turned = jnp.where(
        lane % ROT < ROT // 2,
        pltpu.roll(values, lanes - ROT // 2, 1),
        pltpu.roll(values, ROT // 2, 1),
    )
    return values * cos_table + turned * sine_table


def head_mask(value, head, heads):
    lane = lax.broadcasted_iota(jnp.int32, value.shape, 1)
    return (lane // (value.shape[1] // heads)) == head


def allowed_block(first_row, rows, keys, lower):
    row = lax.broadcasted_iota(jnp.int32, (rows, keys), 0) + first_row
    col = lax.broadcasted_iota(jnp.int32, (rows, keys), 1)
    return (col <= row) & (col >= lower)


def store_shards(place, tz, outs, group, cols, value):
    rows = value.shape[0] // tz
    for b in range(tz):
        outs[group][rows_at((place[1] ^ b) * rows, rows), cols] = value[
            b * rows : (b + 1) * rows
        ].astype(BF)


def forward_body(tz, dp, count, sizes, *refs):
    length, width, nq, nf, nd = sizes
    heads = nd // HD
    place, table, gains, shift_qkv, shift_fc1 = refs[:5]
    at = 5
    shards, pieces_w = refs[at : at + 2 * tz], refs[at + 2 * tz : at + 2 * tz + count]
    at += 2 * tz + count
    out_own, out_sib, x, cot, w, n1, n2, qkv, lse, aa, dgelu, stats = refs[at : at + 12]
    hid, x_sems, w_sems, cot_sems = refs[at + 12 :]
    rows = length // tz
    size = width // dp
    x_in = start_all(
        [
            (one.at[0:rows], x.at[rows_at(shard_rows(place, tz, rows, i), rows)])
            for i, one in enumerate(shards)
        ],
        x_sems,
    )
    parts_w = [
        one.at[j * size : (j + 1) * size] for one in pieces_w for j in range(one.shape[0] // size)
    ]
    w_in = start_all(
        [(one, w.at[rows_at(weight_rows(place, size, i), size)]) for i, one in enumerate(parts_w)],
        w_sems,
    )
    cot_in = start_all(
        [
            (one.at[rows : 2 * rows], cot.at[rows_at(shard_rows(place, tz, rows, i), rows)])
            for i, one in enumerate(shards)
        ],
        cot_sems,
    )
    for i in range(2 * tz):
        x_in[i].wait()
        start = shard_rows(place, tz, rows, i)

        def norm_rows(j, _):
            there = rows_at(start + j * CHUNK, CHUNK)
            value = x[there, :].astype(F32)
            mean = jnp.mean(value, axis=1, keepdims=True)
            center = value - mean
            spread = lax.rsqrt(jnp.mean(center * center, axis=1, keepdims=True) + EPS)
            scaled = center * spread
            n1[there, :] = (scaled * gains[0:1, :] + gains[1:2, :]).astype(BF)
            n2[there, :] = (scaled * gains[2:3, :] + gains[3:4, :]).astype(BF)
            lane = lax.broadcasted_iota(jnp.int32, (CHUNK, 128), 1)
            stats[there, :] = jnp.where(lane == 0, mean, spread)
            return 0

        lax.fori_loop(0, rows // CHUNK, norm_rows, 0)
    wait_all(w_in)
    for g in range(2):
        group = slice(g * length, (g + 1) * length)
        cos_table, sine_table = table[group, 0:nd], table[group, nd : 2 * nd]
        projected = dot(n1[group, :], w[:, 0:nq]) + shift_qkv[...]
        qkv[group, 0:nd] = rotated(projected[:, 0:nd], cos_table, sine_table).astype(BF)
        qkv[group, nd : 2 * nd] = rotated(projected[:, nd : 2 * nd], cos_table, sine_table).astype(
            BF
        )
        qkv[group, 2 * nd : 3 * nd] = projected[:, 2 * nd : 3 * nd].astype(BF)
        hid[...] = dot(n2[group, :], w[:, nq : nq + nf]) + shift_fc1[...]

        def gelu_rows(i, _):
            here = rows_at(i * CHUNK, CHUNK)
            there = rows_at(g * length + i * CHUNK, CHUNK)
            h = hid[here, :]
            phi = 0.5 * (1.0 + lax.erf(h * 0.7071067811865476))
            aa[there, nd : nd + nf] = (h * phi).astype(BF)
            dgelu[there, :] = (phi + h * (0.3989422804014327 * jnp.exp(-0.5 * h * h))).astype(BF)
            return 0

        lax.fori_loop(0, length // CHUNK, gelu_rows, 0)

        half = length // 2
        for block in range(2):
            keys = (block + 1) * half
            q_rows = slice(g * length + block * half, g * length + (block + 1) * half)
            k_rows = slice(g * length, g * length + keys)
            q = qkv[q_rows, 0:nd]
            k = qkv[k_rows, nd : 2 * nd]
            v = qkv[k_rows, 2 * nd : 3 * nd]
            lower = table[q_rows, 2 * nd : 2 * nd + 1].astype(jnp.int32)
            allowed = allowed_block(block * half, half, keys, lower)
            gathered = jnp.zeros((half, nd), F32)
            kept = jnp.zeros((half, 128), F32)
            lane = lax.broadcasted_iota(jnp.int32, (half, 128), 1)
            for h in range(heads):
                mine = head_mask(q, h, heads)
                scores = dot_nt(jnp.where(mine, q, jnp.zeros_like(q)), k) * HD ** (-0.5)
                scores = jnp.where(allowed, scores, -jnp.inf)
                top = jnp.max(scores, axis=1, keepdims=True)
                raised = jnp.exp(scores - top)
                total = jnp.sum(raised, axis=1, keepdims=True)
                soft = (raised * (1.0 / total)).astype(BF)
                gathered = jnp.where(mine, dot(soft, v), gathered)
                kept = jnp.where(lane == h, top + jnp.log(total), kept)
            valid = table[q_rows, 2 * nd + 64 : 2 * nd + 65]
            aa[q_rows, 0:nd] = (gathered * valid).astype(BF)
            lse[q_rows, :] = kept

        quarter = width // 4
        for part in range(4):
            cols = slice(part * quarter, (part + 1) * quarter)
            value = dot_nt(aa[group, :], w[cols, nq + nf :])
            store_shards(place, tz, (out_own, out_sib), g, cols, value)
    wait_all(cot_in)


def second_grads_body(dp, packets, place, aa, cot, *outs):
    grads_out(dp, packets, place, outs, lambda cols: dot_tn(cot[:, cols], aa[...]))


def first_grads_body(dp, packets, nq, place, n1, n2, gg, *outs):
    grads_out(
        dp,
        packets,
        place,
        outs,
        lambda cols: jnp.concatenate(
            [dot_tn(n1[:, cols], gg[:, 0:nq]), dot_tn(n2[:, cols], gg[:, nq:])], axis=1
        ),
    )


def grads_out(dp, packets, place, outs, product):
    size = outs[0].shape[0]
    slots = {i: (out, slot) for out, packet in zip(outs, packets) for slot, i in enumerate(packet)}
    for r in range(dp // 2):
        value = product(slice(2 * r * size, (2 * r + 2) * size)).astype(BF)
        low, high = value[0:size], value[size : 2 * size]
        first = place[0] == 0
        for i, (one, two) in ((2 * r, (low, high)), (2 * r + 1, (high, low))):
            out, slot = slots[i]
            out[slot * size : (slot + 1) * size, :] = jnp.where(first, one, two)


def backward_body(tz, sizes, *refs):
    length, width, nq, nf, nd = sizes
    heads = nd // HD
    place, table, gains, cot, w, qkv, lse, dgelu, stats, x = refs[:10]
    out_own, out_sib, gg, sums, bias_sums = refs[10:15]
    gact, g1, g2, acc, dk, dv = refs[15:]
    rows = length // tz
    acc[...] = jnp.zeros_like(acc)
    bias_sums[...] = jnp.zeros_like(bias_sums)
    for g in range(2):
        group = slice(g * length, (g + 1) * length)
        both = dot(cot[group, :], w[:, nq + nf :])
        grad_out = both[:, 0:nd].astype(BF)
        gact[...] = both[:, nd:]

        def hidden_rows(i, total):
            there = rows_at(g * length + i * CHUNK, CHUNK)
            value = gact[rows_at(i * CHUNK, CHUNK), :] * dgelu[there, :].astype(F32)
            gg[there, nq : nq + nf] = value.astype(BF)
            return total + jnp.sum(value.reshape(CHUNK // 8, 8, nf), axis=0)

        total = lax.fori_loop(0, length // CHUNK, hidden_rows, jnp.zeros((8, nf), F32))
        bias_sums[:, nq : nq + nf] += total

        half = length // 2
        dk[...] = jnp.zeros_like(dk)
        dv[...] = jnp.zeros_like(dv)
        for block in range(2):
            keys = (block + 1) * half
            q_rows = slice(g * length + block * half, g * length + (block + 1) * half)
            k_rows = slice(g * length, g * length + keys)
            q = qkv[q_rows, 0:nd]
            k = qkv[k_rows, nd : 2 * nd]
            v = qkv[k_rows, 2 * nd : 3 * nd]
            go = grad_out[block * half : (block + 1) * half]
            lower = table[q_rows, 2 * nd : 2 * nd + 1].astype(jnp.int32)
            allowed = allowed_block(block * half, half, keys, lower)
            dq = jnp.zeros((half, nd), F32)
            for h in range(heads):
                mine = head_mask(q, h, heads)
                zero = jnp.zeros_like(q)
                q_h = jnp.where(mine, q, zero)
                go_h = jnp.where(mine, go, zero)
                scores = dot_nt(q_h, k) * HD ** (-0.5)
                probs = jnp.exp(jnp.where(allowed, scores - lse[q_rows, h : h + 1], -jnp.inf))
                grad_soft = dot_nt(go_h, v)
                inner = jnp.sum(probs * grad_soft, axis=1, keepdims=True)
                grad_scores = (probs * (grad_soft - inner) * HD ** (-0.5)).astype(BF)
                dq = jnp.where(mine, dot(grad_scores, k), dq)
                dk[0:keys, :] += dot_tn(grad_scores, q_h)
                dv[0:keys, :] += dot_tn(probs.astype(BF), go_h)
            grads_q = rotated(dq, table[q_rows, 0:nd], -table[q_rows, nd : 2 * nd])
            gg[q_rows, 0:nd] = grads_q.astype(BF)
            bias_sums[:, 0:nd] += jnp.sum(grads_q.reshape(half // 8, 8, nd), axis=0)
        grads_k = rotated(dk[...], table[group, 0:nd], -table[group, nd : 2 * nd])
        gg[group, nd : 2 * nd] = grads_k.astype(BF)
        gg[group, 2 * nd : 3 * nd] = dv[...].astype(BF)
        bias_sums[:, nd : 2 * nd] += jnp.sum(grads_k.reshape(length // 8, 8, nd), axis=0)
        bias_sums[:, 2 * nd : 3 * nd] += jnp.sum(dv[...].reshape(length // 8, 8, nd), axis=0)

        quarter = width // 4
        for part in range(4):
            cols = slice(part * quarter, (part + 1) * quarter)
            g1[:, cols] = dot_nt(gg[group, 0:nq], w[cols, 0:nq])
            g2[:, cols] = dot_nt(gg[group, nq:], w[cols, nq : nq + nf])

        out = (out_own, out_sib)[g]
        for r in range(tz):
            start = (place[1] ^ r) * rows

            def back_rows(j, _):
                inside = rows_at(start + j * CHUNK, CHUNK)
                there = rows_at(g * length + start + j * CHUNK, CHUNK)
                scaled = (x[there, :].astype(F32) - stats[there, 0:1]) * stats[there, 1:2]
                one, two = g1[inside, :], g2[inside, :]

                def add(slot, value):
                    acc[slot] += jnp.sum(value.reshape(CHUNK // 8, 8, width), axis=0)

                add(0, one * scaled)
                add(1, one)
                add(2, two * scaled)
                add(3, two)
                out[rows_at(r * rows + j * CHUNK, CHUNK), :] = (
                    one * gains[0:1, :] + two * gains[2:3, :]
                ).astype(BF)
                return 0

            lax.fori_loop(0, rows // CHUNK, back_rows, 0)
    for i in range(4):
        sums[i : i + 1, :] = jnp.sum(acc[i], axis=0, keepdims=True)


def combine_body(tz, place, own, other, *outs):
    rows = own.shape[0] // tz
    for r, out in enumerate(outs):
        at = slice(r * rows, (r + 1) * rows)
        out[...] = (own[at, :].astype(F32) + other[at, :].astype(F32)).astype(out.dtype)


def by_kind(values, heads):
    parts = [
        values[..., (h * 3 + kind) * HD : (h * 3 + kind + 1) * HD]
        for kind in range(3)
        for h in range(heads)
    ]
    return jnp.concatenate(parts, axis=-1)


def by_head(values, heads):
    parts = [
        values[..., (kind * heads + h) * HD : (kind * heads + h + 1) * HD]
        for h in range(heads)
        for kind in range(3)
    ]
    return jnp.concatenate(parts, axis=-1)


def pack_body(sizes, place, qkv_in, fc1_in, dense_in, fc2_in, kept, given, *scratch):
    nq, nf, nd = sizes
    qkv, fc1, dense, fc2, sems = scratch
    wait_all(
        start_all([(qkv_in, qkv), (fc1_in, fc1), (dense_in, dense), (fc2_in, fc2)], sems)
    )
    for out, which in ((given, 1 - place[0]), (kept, place[0])):

        def half(ref, size):
            return ref[:, pl.ds(pl.multiple_of(which * size, size), size)]

        out[:, 0:nq] = by_kind(half(qkv, nq), nd // HD)
        out[:, nq : nq + nf] = half(fc1, nf)
        out[:, nq + nf : nq + nf + nd] = half(dense, nd)
        out[:, nq + nf + nd :] = half(fc2, nf)


def halves_body(place, one, two, first, last, sems):
    size = one.shape[0] // 2
    wait_all(start_all([(one.at[0:size], first), (two.at[size : 2 * size], last)], sems))


def messages_body(place, to_x, to_y, from_y, from_x, out_x, out_y):
    size = to_x.shape[0]
    out_x[...] = to_x[...] + from_y[size : 2 * size, :]
    out_y[...] = to_y[...] + from_x[size : 2 * size, :]


def split_body(tz, place, own, other, mine, from_x, from_y, *outs):
    combine_body(tz, place, own, other, *outs[:tz])
    shard_sum(mine, from_x, from_y, outs[tz])


def shard_sum(mine, first, second, out):
    size = out.shape[0]
    out[...] = (
        mine[...].astype(F32) + first[0:size, :].astype(F32) + second[...].astype(F32)
    ).astype(BF)


def relay_body(place, shard, passed, to_x, to_y, from_y, from_x, sums, others, *outs):
    out_shard, out_x, out_y, out_sums = outs
    keep = (place[2] == 1).astype(F32)
    out_shard[...] = (shard[...].astype(F32) + keep * passed[...].astype(F32)).astype(BF)
    messages_body(place, to_x, to_y, from_y, from_x, out_x, out_y)
    out_sums[...] = sums[...] + others[...]


def finish_body(place, own, first, second, across, rows, mine, from_x, from_y, sums, others, *outs):
    out_rows, out_shard, out_sums = outs
    size = own.shape[0]
    keep = (place[2] == 1).astype(F32)
    back = (
        own[...]
        + first[...].astype(F32)
        + second[...].astype(F32)
        + keep * across[...].astype(F32)
    )
    value = rows[0:size, :].astype(F32)
    center = value - jnp.mean(value, axis=1, keepdims=True)
    spread = lax.rsqrt(jnp.mean(center * center, axis=1, keepdims=True) + EPS)
    scaled = center * spread
    out_rows[...] = rows[size : 2 * size, :].astype(F32) + spread * (
        back
        - jnp.mean(back, axis=1, keepdims=True)
        - scaled * jnp.mean(back * scaled, axis=1, keepdims=True)
    )
    shard_sum(mine, from_x, from_y, out_shard)
    out_sums[...] = sums[...] + others[...]


def join_body(heads, widths, count, place, *refs):
    parts, other, outs = refs[:count], refs[count], refs[count + 1 :]
    rows = other.shape[0]
    total = parts[0][0:rows, :].astype(F32)
    for one in parts[1:]:
        total = total + one[0:rows, :].astype(F32)
    for half, which in ((total, place[0]), (other[...].astype(F32), 1 - place[0])):
        at = 0
        for i, (out, size) in enumerate(zip(outs, widths)):
            value = half[:, at : at + size]
            if i == 0 and heads:
                value = by_head(value, heads)
            out[:, pl.ds(pl.multiple_of(which * size, size), size)] = value
            at += size


def xor_pairs(size, flip):
    return [(i, i ^ flip) for i in range(size)]


def on_device(
    dp,
    tz,
    inputs,
    segment_ids,
    ln1_gain,
    ln1_bias,
    ln2_gain,
    ln2_bias,
    qkv_weight,
    qkv_bias,
    dense_weight,
    dense_bias,
    fc1_weight,
    fc1_bias,
    fc2_weight,
    fc2_bias,
    cotangent,
):
    rows, width = inputs.shape
    length = segment_ids.shape[0]
    tokens = 2 * length
    chips = dp // 2
    here = lax.axis_index("dp")
    core = here % 2
    chip = here // 2
    tensor = lax.axis_index("tensor")
    step = width // chips
    nq, nf, nd = qkv_weight.shape[1] // 2, fc1_weight.shape[1] // 2, dense_weight.shape[1] // 2
    wide = nq + nf + nd + nf
    heads = nd // HD
    sizes = (length, width, nq, nf, nd)
    middle = (tensor == 1) | (tensor == 2)
    place = jnp.stack([core, tensor, middle]).astype(jnp.int32)

    def turn(values):
        parts = [
            lax.dynamic_slice_in_dim(values, (chip ^ r) * step, step, axis=values.ndim - 1)
            for r in range(chips)
        ]
        return jnp.concatenate(parts, axis=-1)

    def sibling(values):
        return lax.ppermute(values, "dp", xor_pairs(dp, 1))

    def over_chip(values, flip):
        return lax.ppermute(values, "dp", xor_pairs(dp, 2 * flip))

    def over_tensor(values, flip):
        return lax.ppermute(values, "tensor", xor_pairs(tz, flip))

    def together(*values):
        return lax.optimization_barrier(values)

    def after(values, event):
        return lax.optimization_barrier((values, event))[0]

    def over_middle(values):
        return lax.ppermute(values, "tensor", [(0, 0), (1, 2), (2, 1), (3, 3)])

    def add_sibling(place, own, other):
        dtypes = [F32] + [BF] * (tz - 1)
        return kernel_call(
            partial(combine_body, tz),
            "add_sibling",
            [shape((rows, width), d) for d in dtypes],
            (place, own, other),
            [],
            LITTLE,
        )

    def added(parts):
        total = parts[0]
        for one in parts[1:]:
            total = total + one.astype(F32)
        return total

    def gather(kept, given, own_rows):
        given, own_rows = together(sibling(given), own_rows)
        if chips != 4 or tz != 4:
            blocks = [(kept, given)]
            flip = 1
            while flip < chips:
                blocks = blocks + [(over_chip(a, flip), over_chip(b, flip)) for a, b in blocks]
                flip *= 2
            shards = [own_rows] + [over_tensor(own_rows, r) for r in range(1, tz)]
            return [one for block in blocks for one in block], shards + [
                sibling(one) for one in shards
            ]
        pair = jnp.concatenate([kept, given], axis=0)
        second, first, from_x, from_y, sib_own = together(
            over_tensor(own_rows, 2),
            over_tensor(own_rows, 1),
            over_chip(pair, 1),
            over_chip(pair, 2),
            sibling(own_rows),
        )
        to_y, to_x = kernel_call(
            halves_body,
            "halves",
            [shape(kept.shape, BF)] * 2,
            (place,),
            [pltpu.SemaphoreType.DMA((2,))],
            LITTLE,
            (from_x, from_y),
            True,
        )
        across, relayed, far_own, far_other, sib_second = together(
            over_middle(own_rows),
            over_tensor(second, 1),
            over_chip(to_y, 2),
            over_chip(to_x, 1),
            sibling(second),
        )
        third = jnp.where(middle, across, relayed)
        return [kept, given, from_x, from_y, far_own, far_other], [
            own_rows,
            first,
            second,
            third,
            sib_own,
            sibling(first),
            sib_second,
            sibling(third),
        ]

    rounds = chips == 4 and tz == 4
    packets = [[0], [1], [4, 6], [3, 7], [2], [5]] if rounds else [[i] for i in range(dp)]

    def first_round(parts):
        if rounds:
            return [over_chip(parts[2], 2), over_chip(parts[3], 1)]
        return []

    def chip_sums(parts):
        blocks = [(parts[2 * r], parts[2 * r + 1]) for r in range(chips)]
        flip = chips // 2
        while flip:
            blocks = [
                tuple(
                    (a.astype(F32) + over_chip(b, flip).astype(F32)).astype(BF)
                    for a, b in zip(blocks[r], blocks[r + flip])
                )
                for r in range(flip)
            ]
            flip //= 2
        return blocks[0]

    def join(terms, other, widths, own_heads):
        return kernel_call(
            partial(join_body, own_heads, widths, len(terms)),
            "join_halves",
            [shape((width // dp, 2 * one), F32) for one in widths],
            (place, *terms, other),
            [],
            LITTLE,
        )

    def half_of(values, which):
        size = values.shape[-1] // 2
        return lax.dynamic_slice_in_dim(values, which * size, size, axis=values.ndim - 1)


    kept, given = kernel_call(
        partial(pack_body, (nq, nf, nd)),
        "pack_weights",
        [shape((width // dp, wide), BF)] * 2,
        (place,),
        [
            pltpu.VMEM(one.shape, BF) for one in (qkv_weight, fc1_weight, dense_weight, fc2_weight)
        ]
        + [pltpu.SemaphoreType.DMA((4,))],
        LITTLE,
        (qkv_weight, fc1_weight, dense_weight, fc2_weight),
    )

    own_rows = turn(after(inputs, kept))
    own_validity = lax.dynamic_slice_in_dim(segment_ids, tensor * rows, rows) >= 0
    masked = jnp.where(own_validity[:, None], turn(cotangent), jnp.zeros((), BF))
    weights, shards = gather(kept, given, jnp.concatenate([own_rows, masked], axis=0))

    both_ids = jnp.stack([segment_ids, sibling(segment_ids)])
    earlier = (both_ids[:, None, :] >= 0) & (both_ids[:, None, :] < both_ids[:, :, None])
    begins = jnp.sum(earlier.astype(jnp.int32), axis=2).reshape(tokens)
    flat_ids = both_ids.reshape(tokens)
    index = jnp.arange(tokens, dtype=jnp.int32) % length
    position = (index - begins).astype(F32)
    lane = jnp.arange(nd, dtype=jnp.int32) % HD
    half_rot = ROT // 2
    frequency = jnp.where(
        lane < ROT, 10000.0 ** (-2.0 * (lane % half_rot).astype(F32) / ROT), 0.0
    )
    angles = position[:, None] * frequency[None, :]
    sign = jnp.where(lane < half_rot, -1.0, 1.0)
    lower = jnp.where(flat_ids >= 0, begins, index).astype(F32)
    valid = (flat_ids >= 0).astype(F32)
    last = jnp.where(jnp.arange(128)[None, :] < 64, lower[:, None], valid[:, None])
    table = jnp.concatenate([jnp.cos(angles), jnp.sin(angles) * sign, last], axis=1)

    gains = turn(jnp.stack([ln1_gain, ln1_bias, ln2_gain, ln2_bias]))
    shift_qkv = by_kind(half_of(qkv_bias, core), heads)[None, :]
    shift_fc1 = half_of(fc1_bias, core)[None, :]

    part_own, part_sib, x, cot, w, n1, n2, qkv, lse, aa, dgelu, stats = kernel_call(
        partial(forward_body, tz, dp, len(weights), sizes),
        "forward",
        [
            shape((length, width), BF),
            shape((length, width), BF),
            shape((tokens, width), BF),
            shape((tokens, width), BF),
            shape((width, wide), BF),
            shape((tokens, width), BF),
            shape((tokens, width), BF),
            shape((tokens, nq), BF),
            shape((tokens, 128), F32),
            shape((tokens, nd + nf), BF),
            shape((tokens, nf), BF),
            shape((tokens, 128), F32),
        ],
        (place, table, gains, shift_qkv, shift_fc1),
        [
            pltpu.VMEM((length, nf), F32),
            pltpu.SemaphoreType.DMA((2 * tz,)),
            pltpu.SemaphoreType.DMA((dp,)),
            pltpu.SemaphoreType.DMA((2 * tz,)),
        ],
        16,
        (*shards, *weights),
    )

    part_other = sibling(part_sib)
    second_parts = kernel_call(
        partial(second_grads_body, dp, packets),
        "second_grads",
        [shape((width // dp * len(packet), nd + nf), BF) for packet in packets],
        (place, aa, cot),
        [],
        LITTLE,
    )
    branch_shards = add_sibling(after(place, second_parts[0]), part_own, part_other)

    branch_moved = [over_tensor(branch_shards[r], r) for r in range(1, tz)]
    second_first = first_round(second_parts)
    back_own, back_sib, gg, sums, bias_sums = kernel_call(
        partial(backward_body, tz, sizes),
        "backward",
        [
            shape((length, width), BF),
            shape((length, width), BF),
            shape((tokens, nq + nf), BF),
            shape((4, width), F32),
            shape((8, nq + nf), F32),
        ],
        (
            after(place, branch_shards[1]),
            table,
            gains,
            cot,
            w,
            qkv,
            lse,
            dgelu,
            stats,
            x,
        ),
        [
            pltpu.VMEM((length, nf), F32),
            pltpu.VMEM((length, width), F32),
            pltpu.VMEM((length, width), F32),
            pltpu.VMEM((4, 8, width), F32),
            pltpu.VMEM((length, nd), F32),
            pltpu.VMEM((length, nd), F32),
        ],
        14,
    )
    first_parts = kernel_call(
        partial(first_grads_body, dp, packets, nq),
        "first_grads",
        [shape((width // dp * len(packet), nq + nf), BF) for packet in packets],
        (place, n1, n2, gg),
        [],
        LITTLE,
    )
    back_sib, sums, bias_sums = after(
        (back_sib, sums, bias_sums), (branch_moved, second_first, first_parts[0])
    )
    output = (
        inputs.astype(F32)
        + turn(added([branch_shards[0]] + branch_moved))
        + dense_bias
        + fc2_bias
    ).astype(BF)

    out_bias = jnp.sum(masked.astype(F32), axis=0, keepdims=True)
    sums = turn(jnp.concatenate([sums, out_bias], axis=0))
    bias_part = jnp.sum(bias_sums, axis=0)
    biases = jnp.zeros((2 * width,), F32)
    biases = lax.dynamic_update_slice_in_dim(biases, by_head(bias_part[:nq], heads), core * nq, 0)
    biases = lax.dynamic_update_slice_in_dim(biases, bias_part[nq:], width + core * nf, 0)
    sums = jnp.concatenate([sums, biases.reshape(2, width)], axis=0)

    if rounds:
        now = after(place, (branch_moved, second_first, first_parts[0]))
        second_messages = kernel_call(
            messages_body,
            "second_messages",
            [shape(second_parts[4].shape, BF)] * 2,
            (now, second_parts[4], second_parts[5], *second_first),
            [],
            LITTLE,
        )
        second_x, second_y = over_chip(second_messages[0], 1), over_chip(second_messages[1], 2)
        back_other = sibling(back_sib)
        first_first = first_round(first_parts)
        sums_core = sibling(sums)
        *back_shards, second_other = kernel_call(
            partial(split_body, tz),
            "split_back",
            [shape((rows, width), F32)]
            + [shape((rows, width), BF)] * 3
            + [shape(second_parts[1].shape, BF)],
            (place, back_own, back_other, second_parts[1], second_first[1], second_y),
            [],
            LITTLE,
        )
        sums = sums + sums_core
        passed, across = over_tensor(back_shards[3], 1), over_middle(back_shards[3])
        sums_x = over_chip(sums, 1)
        second_sib = sibling(second_other)
        now = after(place, (across, second_sib))
        shard, first_x, first_y, sums = kernel_call(
            relay_body,
            "second_round",
            [
                shape((rows, width), BF),
                shape(first_parts[4].shape, BF),
                shape(first_parts[5].shape, BF),
                shape(sums.shape, F32),
            ],
            (
                now,
                back_shards[2],
                passed,
                first_parts[4],
                first_parts[5],
                *first_first,
                sums,
                sums_x,
            ),
            [],
            LITTLE,
        )
        back_second, back_first = over_tensor(shard, 2), over_tensor(back_shards[1], 1)
        first_x, first_y = over_chip(first_x, 1), over_chip(first_y, 2)
        sums_y = over_chip(sums, 2)
        input_grad, first_other, sums = kernel_call(
            finish_body,
            "finish_rows",
            [
                shape((rows, width), F32),
                shape(first_parts[1].shape, BF),
                shape(sums.shape, F32),
            ],
            (
                place,
                back_shards[0],
                back_first,
                back_second,
                across,
                shards[0],
                first_parts[1],
                first_first[1],
                first_y,
                sums,
                sums_y,
            ),
            [],
            LITTLE,
        )
        first_terms = [first_parts[0], first_first[0], first_x]
        second_terms = [second_parts[0], second_first[0], second_x]
        first_sib = sibling(first_other)
    else:
        back = added(
            [
                one if r == 0 else over_tensor(one, r)
                for r, one in enumerate(add_sibling(place, back_own, sibling(back_sib)))
            ]
        )
        value = own_rows.astype(F32)
        center = value - jnp.mean(value, axis=1, keepdims=True)
        spread = lax.rsqrt(jnp.mean(center * center, axis=1, keepdims=True) + EPS)
        scaled = center * spread
        input_grad = masked.astype(F32) + spread * (
            back
            - jnp.mean(back, axis=1, keepdims=True)
            - scaled * jnp.mean(back * scaled, axis=1, keepdims=True)
        )
        (second_own, second_other), (first_own, first_other) = (
            chip_sums(second_parts),
            chip_sums(first_parts),
        )
        second_terms, first_terms = [second_own], [first_own]
        second_sib, first_sib = sibling(second_other), sibling(first_other)
        flip = 1
        while flip < dp:
            sums = sums + lax.ppermute(sums, "dp", xor_pairs(dp, flip))
            flip *= 2
    input_grad = turn(input_grad)
    dense_grad, fc2_grad = join(second_terms, second_sib, (nd, nf), 0)
    qkv_grad, fc1_grad = join(first_terms, first_sib, (nq, nf), heads)
    biases = sums[5:]
    sums = added([sums[:5]] + [over_tensor(sums[:5], r) for r in range(1, tz)])

    return (
        output,
        input_grad,
        sums[0],
        sums[1],
        sums[2],
        sums[3],
        qkv_grad,
        biases[0, : 2 * nq],
        dense_grad,
        sums[4],
        fc1_grad,
        biases[1, : 2 * nf],
        fc2_grad,
        sums[4],
    )


def solution(mesh):
    return jax.shard_map(
        partial(on_device, mesh.shape["dp"], mesh.shape["tensor"]),
        mesh=mesh,
        in_specs=(
            P(("dp", "tensor"), None),
            P("dp"),
            P(),
            P(),
            P(),
            P(),
            P("dp", "tensor"),
            P("tensor"),
            P("dp", "tensor"),
            P(),
            P("dp", "tensor"),
            P("tensor"),
            P("dp", "tensor"),
            P(),
            P(("dp", "tensor"), None),
        ),
        out_specs=(
            P(("dp", "tensor"), None),
            P(("dp", "tensor"), None),
            P(),
            P(),
            P(),
            P(),
            P("dp", "tensor"),
            P("tensor"),
            P("dp", "tensor"),
            P(),
            P("dp", "tensor"),
            P("tensor"),
            P("dp", "tensor"),
            P(),
        ),
        check_vma=False,
    )
```

```python
from functools import partial

import jax
import jax.numpy as jnp
from jax import lax
from jax.experimental import pallas as pl
from jax.experimental.pallas import tpu as pltpu
from jax.sharding import PartitionSpec as P

HD = 64
ROT = 16
EPS = 1e-05
SCALE = HD**-0.5
BF = jnp.bfloat16
F32 = jnp.float32
LN_ROWS = 128
ANY = pl.BlockSpec(memory_space=pl.ANY)
HBM = pl.BlockSpec(memory_space=pltpu.HBM)
VMEM = pl.BlockSpec(memory_space=pltpu.VMEM)
SMEM = pl.BlockSpec(memory_space=pltpu.SMEM)
VMEM_LIMIT = 16 * 1024 * 1024
PEAK = 1.15e9
LITTLE = 0.01


def dot(a, b):
    return jnp.dot(a, b, preferred_element_type=F32)


def dot_nt(a, b):
    return lax.dot_general(a, b, (((1,), (1,)), ((), ())), preferred_element_type=F32)


def dot_tn(a, b):
    return lax.dot_general(a, b, (((0,), (0,)), ((), ())), preferred_element_type=F32)


def shape(dims, dtype):
    return jax.ShapeDtypeStruct(dims, dtype)


def kernel_call(body, name, outs, operands, scratch, micros, fetched=(), placed=False):
    return pl.pallas_call(
        body,
        name=name,
        out_shape=outs,
        in_specs=[SMEM] + [VMEM] * (len(operands) - 1) + [HBM] * len(fetched),
        out_specs=[ANY if placed else VMEM] * len(outs),
        scratch_shapes=scratch,
        cost_estimate=pl.CostEstimate(
            flops=int(micros * PEAK), bytes_accessed=0, transcendentals=0
        ),
        compiler_params=pltpu.CompilerParams(vmem_limit_bytes=VMEM_LIMIT),
    )(*operands, *fetched)


def start_all(pairs, sems, first=0):
    copies = [
        pltpu.make_async_copy(src, dst, sems.at[first + i]) for i, (src, dst) in enumerate(pairs)
    ]
    for one in copies:
        one.start()
    return copies


def wait_all(copies):
    for one in copies:
        one.wait()


def rows_at(start, size):
    return pl.ds(pl.multiple_of(start, size), size)


def shard_rows(place, tz, rows, i):
    return i // tz * tz * rows + (place[1] ^ (i % tz)) * rows


def weight_rows(place, size, i):
    return (i - i % 2 + (place[0] ^ (i % 2))) * size


def rotated(values, cos_table, sine_table):
    lane = lax.broadcasted_iota(jnp.int32, values.shape, 1)
    lanes = values.shape[1]
    turned = jnp.where(
        lane % ROT < ROT // 2,
        pltpu.roll(values, lanes - ROT // 2, 1),
        pltpu.roll(values, ROT // 2, 1),
    )
    return values * cos_table + turned * sine_table


def head_mask(value, head, heads):
    lane = lax.broadcasted_iota(jnp.int32, value.shape, 1)
    return (lane // (value.shape[1] // heads)) == head


def allowed_block(first_row, rows, keys, lower):
    row = lax.broadcasted_iota(jnp.int32, (rows, keys), 0) + first_row
    col = lax.broadcasted_iota(jnp.int32, (rows, keys), 1)
    return (col <= row) & (col >= lower)


def store_shards(place, tz, outs, group, cols, value):
    rows = value.shape[0] // tz
    for b in range(tz):
        outs[group][rows_at((place[1] ^ b) * rows, rows), cols] = value[
            b * rows : (b + 1) * rows
        ].astype(BF)


def forward_body(tz, dp, count, sizes, *refs):
    length, width, nq, nf, nd = sizes
    heads = nd // HD
    place, table, gains, shift_qkv, shift_fc1 = refs[:5]
    at = 5
    shards, pieces_w = refs[at : at + 2 * tz], refs[at + 2 * tz : at + 2 * tz + count]
    at += 2 * tz + count
    out_own, out_sib, x, w, n1, n2, qkv, lse, aa, dgelu, stats = refs[at : at + 11]
    x_sems, w_sems = refs[at + 11 :]
    rows = length // tz
    size = width // dp
    x_in = start_all(
        [
            (one, x.at[rows_at(shard_rows(place, tz, rows, i), rows)])
            for i, one in enumerate(shards)
        ],
        x_sems,
    )
    parts_w = [
        one.at[j * size : (j + 1) * size] for one in pieces_w for j in range(one.shape[0] // size)
    ]
    w_in = start_all(
        [(one, w.at[rows_at(weight_rows(place, size, i), size)]) for i, one in enumerate(parts_w)],
        w_sems,
    )
    for i in range(2 * tz):
        x_in[i].wait()
        start = shard_rows(place, tz, rows, i)

        for j in range(rows // LN_ROWS):
            there = rows_at(start + j * LN_ROWS, LN_ROWS)
            value = x[there, :].astype(F32)
            mean = jnp.mean(value, axis=1, keepdims=True)
            center = value - mean
            spread = lax.rsqrt(jnp.mean(center * center, axis=1, keepdims=True) + EPS)
            scaled = center * spread
            n1[there, :] = (scaled * gains[0:1, :] + gains[1:2, :]).astype(BF)
            n2[there, :] = (scaled * gains[2:3, :] + gains[3:4, :]).astype(BF)
            lane = lax.broadcasted_iota(jnp.int32, (LN_ROWS, 128), 1)
            stats[there, :] = jnp.where(lane == 0, mean, spread)
    wait_all(w_in)
    for g in range(2):
        group = slice(g * length, (g + 1) * length)
        cos_table, sine_table = table[group, 0:nd], table[group, nd : 2 * nd]
        projected = dot(n1[group, :], w[:, 0:nq]) + shift_qkv[...]
        qkv[group, 0:nd] = rotated(projected[:, 0:nd], cos_table, sine_table).astype(BF)
        qkv[group, nd : 2 * nd] = rotated(projected[:, nd : 2 * nd], cos_table, sine_table).astype(
            BF
        )
        qkv[group, 2 * nd : 3 * nd] = projected[:, 2 * nd : 3 * nd].astype(BF)
        for part in range(2):
            cols = slice(part * nf // 2, (part + 1) * nf // 2)
            h = dot(n2[group, :], w[:, nq + cols.start : nq + cols.stop]) + shift_fc1[:, cols]
            phi = 0.5 * (1.0 + lax.erf(h * 0.7071067811865476))
            aa[group, nd + cols.start : nd + cols.stop] = (h * phi).astype(BF)
            dgelu[group, cols] = (phi + h * (0.3989422804014327 * jnp.exp(-0.5 * h * h))).astype(BF)

        half = length // 2
        for block in range(2):
            keys = (block + 1) * half
            q_rows = slice(g * length + block * half, g * length + (block + 1) * half)
            k_rows = slice(g * length, g * length + keys)
            q = qkv[q_rows, 0:nd] * SCALE
            k = qkv[k_rows, nd : 2 * nd]
            v = qkv[k_rows, 2 * nd : 3 * nd]
            lower = table[q_rows, 2 * nd : 2 * nd + 1].astype(jnp.int32)
            allowed = allowed_block(block * half, half, keys, lower)
            gathered = jnp.zeros((half, nd), F32)
            kept = jnp.zeros((half, 128), F32)
            lane = lax.broadcasted_iota(jnp.int32, (half, 128), 1)
            for h in range(heads):
                mine = head_mask(q, h, heads)
                scores = dot_nt(jnp.where(mine, q, jnp.zeros_like(q)), k)
                scores = jnp.where(allowed, scores, -jnp.inf)
                top = jnp.max(scores, axis=1, keepdims=True)
                raised = jnp.exp(scores - top)
                total = jnp.sum(raised, axis=1, keepdims=True)
                soft = (raised * (1.0 / total)).astype(BF)
                gathered = jnp.where(mine, dot(soft, v), gathered)
                kept = jnp.where(lane == h, top + jnp.log(total), kept)
            valid = table[q_rows, 2 * nd + 64 : 2 * nd + 65]
            aa[q_rows, 0:nd] = (gathered * valid).astype(BF)
            lse[q_rows, :] = kept

        quarter = width // 4
        for part in range(4):
            cols = slice(part * quarter, (part + 1) * quarter)
            value = dot_nt(aa[group, :], w[cols, nq + nf :])
            store_shards(place, tz, (out_own, out_sib), g, cols, value)


def second_grads_body(tz, dp, packets, place, aa, *refs):
    shards, cot, outs, sems = refs[: 2 * tz], refs[2 * tz], refs[2 * tz + 1 : -1], refs[-1]
    rows = shards[0].shape[0]
    wait_all(
        start_all(
            [
                (one, cot.at[rows_at(shard_rows(place, tz, rows, i), rows)])
                for i, one in enumerate(shards)
            ],
            sems,
        )
    )
    grads_out(dp, packets, place, outs, lambda cols: dot_tn(cot[:, cols], aa[...]))


def first_grads_body(dp, packets, nq, place, n1, n2, gg, *outs):
    grads_out(
        dp,
        packets,
        place,
        outs,
        lambda cols: jnp.concatenate(
            [dot_tn(n1[:, cols], gg[:, 0:nq]), dot_tn(n2[:, cols], gg[:, nq:])], axis=1
        ),
    )


def grads_out(dp, packets, place, outs, product):
    size = outs[0].shape[0]
    slots = {i: (out, slot) for out, packet in zip(outs, packets) for slot, i in enumerate(packet)}
    for r in range(dp // 2):
        value = product(slice(2 * r * size, (2 * r + 2) * size)).astype(BF)
        low, high = value[0:size], value[size : 2 * size]
        first = place[0] == 0
        for i, (one, two) in ((2 * r, (low, high)), (2 * r + 1, (high, low))):
            out, slot = slots[i]
            out[slot * size : (slot + 1) * size, :] = jnp.where(first, one, two)


def eight_rows(value):
    rows, columns = value.shape
    return jnp.sum(value.reshape(rows // 8, 8, columns), axis=0)


def backward_body(tz, chips, sizes, *refs):
    length, width, nq, nf, nd = sizes
    heads = nd // HD
    place, table, gains, cot, w, qkv, lse, dgelu, stats, x = refs[:10]
    out_own, out_sib, gg, sums = refs[10:14]
    acc, dk, dv, bias_sums = refs[14:]
    rows = length // tz
    acc[...] = jnp.zeros_like(acc)
    bias_sums[...] = jnp.zeros_like(bias_sums)
    for g in range(2):
        group = slice(g * length, (g + 1) * length)
        grad_out = dot(cot[group, :], w[:, nq + nf : nq + nf + nd]).astype(BF)
        for part in range(2):
            cols = slice(part * nf // 2, (part + 1) * nf // 2)
            value = dot(cot[group, :], w[:, nq + nf + nd + cols.start : nq + nf + nd + cols.stop])
            value = value * dgelu[group, cols].astype(F32)
            gg[group, nq + cols.start : nq + cols.stop] = value.astype(BF)
            bias_sums[:, nq + cols.start : nq + cols.stop] += eight_rows(value)

        half = length // 2
        dk[...] = jnp.zeros_like(dk)
        dv[...] = jnp.zeros_like(dv)
        for block in range(2):
            keys = (block + 1) * half
            q_rows = slice(g * length + block * half, g * length + (block + 1) * half)
            k_rows = slice(g * length, g * length + keys)
            q = qkv[q_rows, 0:nd] * SCALE
            k = qkv[k_rows, nd : 2 * nd]
            v = qkv[k_rows, 2 * nd : 3 * nd]
            k_scaled = k * SCALE
            go = grad_out[block * half : (block + 1) * half]
            lower = table[q_rows, 2 * nd : 2 * nd + 1].astype(jnp.int32)
            allowed = allowed_block(block * half, half, keys, lower)
            dq = jnp.zeros((half, nd), F32)
            for h in range(heads):
                mine = head_mask(q, h, heads)
                zero = jnp.zeros_like(q)
                q_h = jnp.where(mine, q, zero)
                go_h = jnp.where(mine, go, zero)
                scores = dot_nt(q_h, k)
                probs = jnp.exp(jnp.where(allowed, scores - lse[q_rows, h : h + 1], -jnp.inf))
                grad_soft = dot_nt(go_h, v)
                inner = jnp.sum(probs * grad_soft, axis=1, keepdims=True)
                grad_scores = (probs * (grad_soft - inner)).astype(BF)
                dq = jnp.where(mine, dot(grad_scores, k_scaled), dq)
                dk[0:keys, :] += dot_tn(grad_scores, q_h)
                dv[0:keys, :] += dot_tn(probs.astype(BF), go_h)
            grads_q = rotated(dq, table[q_rows, 0:nd], -table[q_rows, nd : 2 * nd])
            gg[q_rows, 0:nd] = grads_q.astype(BF)
            bias_sums[:, 0:nd] += eight_rows(grads_q)
        grads_k = rotated(dk[...], table[group, 0:nd], -table[group, nd : 2 * nd])
        gg[group, nd : 2 * nd] = grads_k.astype(BF)
        gg[group, 2 * nd : 3 * nd] = dv[...].astype(BF)
        bias_sums[:, nd : 2 * nd] += eight_rows(grads_k)
        bias_sums[:, 2 * nd : 3 * nd] += eight_rows(dv[...])

        mean, spread = stats[group, 0:1], stats[group, 1:2]
        quarter = width // 4
        for part in range(4):
            cols = slice(part * quarter, (part + 1) * quarter)
            one = dot_nt(gg[group, 0:nq], w[cols, 0:nq])
            two = dot_nt(gg[group, nq:], w[cols, nq : nq + nf])
            scaled = (x[group, cols].astype(F32) - mean) * spread
            for slot, value in enumerate((one * scaled, one, two * scaled, two)):
                acc[slot, :, cols] += eight_rows(value)
            value = one * gains[0:1, cols] + two * gains[2:3, cols]
            store_shards(place, tz, (out_own, out_sib), g, cols, value)
    sums[...] = jnp.zeros_like(sums)
    own = cot[rows_at(place[1] * rows, rows), :].astype(F32)
    acc[4] = eight_rows(own)
    step = width // chips
    for i in range(5):
        total = jnp.sum(acc[i], axis=0, keepdims=True)
        if step % 128 == 0:
            for r in range(chips):
                at = pl.ds(pl.multiple_of((place[3] ^ r) * step, step), step)
                sums[i : i + 1, at] = total[:, r * step : (r + 1) * step]
        else:
            sums[i : i + 1, :] = total
    total = jnp.sum(bias_sums[...], axis=0, keepdims=True)
    sums[5:6, pl.ds(pl.multiple_of(place[0] * nq, nq), nq)] = by_head(total[:, :nq], heads)
    sums[6:7, pl.ds(pl.multiple_of(place[0] * nf, nf), nf)] = total[:, nq:]
    put_sums(out_sib, length, sums[...])


def put_sums(out, row, value):
    high = value.astype(BF).astype(F32)
    out[row : row + 16, :] = jnp.concatenate([high, value - high], axis=0).astype(BF)


def get_sums(ref, row):
    return ref[row : row + 8, :].astype(F32) + ref[row + 8 : row + 16, :].astype(F32)


def combine_body(tz, place, own, other, *outs):
    rows = own.shape[0] // tz
    for r, out in enumerate(outs):
        at = slice(r * rows, (r + 1) * rows)
        out[0:rows, :] = (own[at, :].astype(F32) + other[at, :].astype(F32)).astype(out.dtype)


def by_kind(values, heads):
    parts = [
        values[..., (h * 3 + kind) * HD : (h * 3 + kind + 1) * HD]
        for kind in range(3)
        for h in range(heads)
    ]
    return jnp.concatenate(parts, axis=-1)


def by_head(values, heads):
    parts = [
        values[..., (kind * heads + h) * HD : (kind * heads + h + 1) * HD]
        for h in range(heads)
        for kind in range(3)
    ]
    return jnp.concatenate(parts, axis=-1)


def pack_body(sizes, place, qkv_in, fc1_in, dense_in, fc2_in, kept, given, *scratch):
    nq, nf, nd = sizes
    qkv, fc1, dense, fc2, sems = scratch
    wait_all(
        start_all([(qkv_in, qkv), (fc1_in, fc1), (dense_in, dense), (fc2_in, fc2)], sems)
    )
    for out, which in ((given, 1 - place[0]), (kept, place[0])):

        def half(ref, size):
            return ref[:, pl.ds(pl.multiple_of(which * size, size), size)]

        out[:, 0:nq] = by_kind(half(qkv, nq), nd // HD)
        out[:, nq : nq + nf] = half(fc1, nf)
        out[:, nq + nf : nq + nf + nd] = half(dense, nd)
        out[:, nq + nf + nd :] = half(fc2, nf)


def messages_body(place, to_x, to_y, from_y, from_x, out_x, out_y):
    size = to_x.shape[0]
    out_x[...] = to_x[...] + from_y[size : 2 * size, :]
    out_y[...] = to_y[...] + from_x[size : 2 * size, :]


def split_body(tz, place, own, other, sums, *outs):
    combine_body(tz, place, own, other, *outs[:tz])
    outs[tz][...] = sums[...] + get_sums(other, own.shape[0])


def shard_sum(mine, first, second, out):
    size = out.shape[0]
    out[...] = (
        mine[...].astype(F32) + first[0:size, :].astype(F32) + second[...].astype(F32)
    ).astype(BF)


def pass_body(place, shard, passed, out):
    rows = shard.shape[0]
    keep = (place[2] == 1).astype(F32)
    out[0:rows, :] = (shard[...].astype(F32) + keep * passed[...].astype(F32)).astype(BF)


def relay_body(place, near, shard, passed, to_x, to_y, from_y, from_x, *refs):
    sums, (out_near, out_shard, out_x, out_y, out_sums) = refs[:-5], refs[-5:]
    rows = near.shape[0]
    total = sums[0][...]
    for one in sums[1:]:
        total = total + one[...]
    out_sums[...] = total
    out_near[0:rows, :] = near[...]
    pass_body(place, shard, passed, out_shard)
    for out in (out_near, out_shard):
        put_sums(out, rows, total)
    messages_body(place, to_x, to_y, from_y, from_x, out_x, out_y)


def other_body(place, mine, first, second, out):
    shard_sum(mine, first, second, out)


def finish_body(place, own, first, second, across, x, cot, sums, third, out_rows, out_sums):
    rows = own.shape[0]
    keep = (place[2] == 1).astype(F32)
    back = (
        own[...]
        + first[0:rows, :].astype(F32)
        + second[0:rows, :].astype(F32)
        + keep * across[...].astype(F32)
    )
    value = x[...].astype(F32)
    center = value - jnp.mean(value, axis=1, keepdims=True)
    spread = lax.rsqrt(jnp.mean(center * center, axis=1, keepdims=True) + EPS)
    scaled = center * spread
    out_rows[...] = cot[...].astype(F32) + spread * (
        back
        - jnp.mean(back, axis=1, keepdims=True)
        - scaled * jnp.mean(back * scaled, axis=1, keepdims=True)
    )
    out_sums[...] = sums[...] + get_sums(first, rows) + get_sums(second, rows) + third[...]


def join_body(heads, widths, count, place, *refs):
    parts, other, outs = refs[:count], refs[count], refs[count + 1 :]
    rows = other.shape[0]
    total = parts[0][0:rows, :].astype(F32)
    for one in parts[1:]:
        total = total + one[0:rows, :].astype(F32)
    for half, which in ((total, place[0]), (other[...].astype(F32), 1 - place[0])):
        at = 0
        for i, (out, size) in enumerate(zip(outs, widths)):
            value = half[:, at : at + size]
            if i == 0 and heads:
                value = by_head(value, heads)
            out[:, pl.ds(pl.multiple_of(which * size, size), size)] = value
            at += size


def xor_pairs(size, flip):
    return [(i, i ^ flip) for i in range(size)]


def on_device(
    dp,
    tz,
    inputs,
    segment_ids,
    ln1_gain,
    ln1_bias,
    ln2_gain,
    ln2_bias,
    qkv_weight,
    qkv_bias,
    dense_weight,
    dense_bias,
    fc1_weight,
    fc1_bias,
    fc2_weight,
    fc2_bias,
    cotangent,
):
    rows, width = inputs.shape
    length = segment_ids.shape[0]
    tokens = 2 * length
    chips = dp // 2
    here = lax.axis_index("dp")
    core = here % 2
    chip = here // 2
    tensor = lax.axis_index("tensor")
    step = width // chips
    nq, nf, nd = qkv_weight.shape[1] // 2, fc1_weight.shape[1] // 2, dense_weight.shape[1] // 2
    wide = nq + nf + nd + nf
    heads = nd // HD
    sizes = (length, width, nq, nf, nd)
    middle = (tensor == 1) | (tensor == 2)
    place = jnp.stack([core, tensor, middle, chip]).astype(jnp.int32)

    def turn(values):
        parts = [
            lax.dynamic_slice_in_dim(values, (chip ^ r) * step, step, axis=values.ndim - 1)
            for r in range(chips)
        ]
        return jnp.concatenate(parts, axis=-1)

    def sibling(values):
        return lax.ppermute(values, "dp", xor_pairs(dp, 1))

    def over_chip(values, flip):
        return lax.ppermute(values, "dp", xor_pairs(dp, 2 * flip))

    def over_tensor(values, flip):
        return lax.ppermute(values, "tensor", xor_pairs(tz, flip))

    def together(*values):
        return lax.optimization_barrier(values)

    def after(values, event):
        return lax.optimization_barrier((values, event))[0]

    def over_middle(values):
        return lax.ppermute(values, "tensor", [(0, 0), (1, 2), (2, 1), (3, 3)])

    def add_sibling(place, own, other):
        dtypes = [F32] + [BF] * (tz - 1)
        return kernel_call(
            partial(combine_body, tz),
            "add_sibling",
            [shape((rows, width), d) for d in dtypes],
            (place, own, other),
            [],
            LITTLE,
        )

    def added(parts):
        total = parts[0]
        for one in parts[1:]:
            total = total + one.astype(F32)
        return total

    def row_tables(arrived):
        both_ids = jnp.stack([segment_ids, sibling(after(segment_ids, arrived))])
        earlier = (both_ids[:, None, :] >= 0) & (both_ids[:, None, :] < both_ids[:, :, None])
        begins = jnp.sum(earlier.astype(jnp.int32), axis=2).reshape(tokens)
        flat_ids = both_ids.reshape(tokens)
        index = jnp.arange(tokens, dtype=jnp.int32) % length
        position = (index - begins).astype(F32)
        lane = jnp.arange(nd, dtype=jnp.int32) % HD
        half_rot = ROT // 2
        frequency = jnp.where(
            lane < ROT, 10000.0 ** (-2.0 * (lane % half_rot).astype(F32) / ROT), 0.0
        )
        angles = position[:, None] * frequency[None, :]
        sign = jnp.where(lane < half_rot, -1.0, 1.0)
        lower = jnp.where(flat_ids >= 0, begins, index).astype(F32)
        valid = (flat_ids >= 0).astype(F32)
        last = jnp.where(jnp.arange(128)[None, :] < 64, lower[:, None], valid[:, None])
        return jnp.concatenate([jnp.cos(angles), jnp.sin(angles) * sign, last], axis=1)

    def gather(kept, given, own_rows, later):
        if chips != 4 or tz != 4:
            blocks = [(kept, sibling(given))]
            flip = 1
            while flip < chips:
                blocks = blocks + [(over_chip(a, flip), over_chip(b, flip)) for a, b in blocks]
                flip *= 2
            shards = [own_rows] + [over_tensor(own_rows, r) for r in range(1, tz)]
            return (
                [one for block in blocks for one in block],
                shards + [sibling(one) for one in shards],
                later,
                row_tables(given),
            )
        moved = [over_tensor(own_rows, r) for r in range(1, tz)]
        kept_x, kept_y, given = together(over_chip(kept, 1), over_chip(kept, 2), sibling(given))
        table = row_tables(kept_x)
        given_x, given_y = over_chip(given, 1), over_chip(given, 2)
        moved, kept_x, given_x, given_y, table = together(moved, kept_x, given_x, given_y, table)
        later = after(later, moved)
        pieces = [kept, given, kept_x, given_x, kept_y, given_y]
        pieces += [over_chip(kept_x, 2), over_chip(given_y, 1)]
        shards = [own_rows] + moved
        return pieces, shards + [sibling(one) for one in shards], later, table

    rounds = chips == 4 and tz == 4
    packets = [[0], [1], [4, 6], [3, 7], [2], [5]] if rounds else [[i] for i in range(dp)]

    def first_round(parts):
        if rounds:
            return [over_chip(parts[2], 2), over_chip(parts[3], 1)]
        return []

    def chip_sums(parts):
        blocks = [(parts[2 * r], parts[2 * r + 1]) for r in range(chips)]
        flip = chips // 2
        while flip:
            blocks = [
                tuple(
                    (a.astype(F32) + over_chip(b, flip).astype(F32)).astype(BF)
                    for a, b in zip(blocks[r], blocks[r + flip])
                )
                for r in range(flip)
            ]
            flip //= 2
        return blocks[0]

    def join(terms, other, widths, own_heads):
        return kernel_call(
            partial(join_body, own_heads, widths, len(terms)),
            "join_halves",
            [shape((width // dp, 2 * one), F32) for one in widths],
            (place, *terms, other),
            [],
            LITTLE,
        )

    def half_of(values, which):
        size = values.shape[-1] // 2
        return lax.dynamic_slice_in_dim(values, which * size, size, axis=values.ndim - 1)


    kept, given = kernel_call(
        partial(pack_body, (nq, nf, nd)),
        "pack_weights",
        [shape((width // dp, wide), BF)] * 2,
        (place,),
        [
            pltpu.VMEM(one.shape, BF) for one in (qkv_weight, fc1_weight, dense_weight, fc2_weight)
        ]
        + [pltpu.SemaphoreType.DMA((4,))],
        LITTLE,
        [
            pltpu.with_memory_space_constraint(one, pltpu.HBM)
            for one in (qkv_weight, fc1_weight, dense_weight, fc2_weight)
        ],
    )

    own_rows = turn(after(inputs, kept))
    own_validity = lax.dynamic_slice_in_dim(segment_ids, tensor * rows, rows) >= 0
    masked = jnp.where(own_validity[:, None], turn(cotangent), jnp.zeros((), BF))
    weights, x_shards, masked, table = gather(kept, given, own_rows, masked)
    c_moved = [over_tensor(masked, r) for r in range(1, tz)]
    masked_sib = sibling(masked)

    gains = turn(jnp.stack([ln1_gain, ln1_bias, ln2_gain, ln2_bias]))
    shift_qkv = by_kind(half_of(qkv_bias, core), heads)[None, :]
    shift_fc1 = half_of(fc1_bias, core)[None, :]

    part_own, part_sib, x, w, n1, n2, qkv, lse, aa, dgelu, stats = kernel_call(
        partial(forward_body, tz, dp, len(weights), sizes),
        "forward",
        [
            shape((length, width), BF),
            shape((length, width), BF),
            shape((tokens, width), BF),
            shape((width, wide), BF),
            shape((tokens, width), BF),
            shape((tokens, width), BF),
            shape((tokens, nq), BF),
            shape((tokens, 128), F32),
            shape((tokens, nd + nf), BF),
            shape((tokens, nf), BF),
            shape((tokens, 128), F32),
        ],
        (after(place, masked_sib), table, gains, shift_qkv, shift_fc1),
        [pltpu.SemaphoreType.DMA((2 * tz,)), pltpu.SemaphoreType.DMA((dp,))],
        LITTLE,
        (*x_shards, *weights),
    )

    c_moved, part_sib = together(c_moved, part_sib)
    branch_shards = add_sibling(place, part_own, sibling(part_sib))
    c_shards = [masked] + c_moved + [masked_sib] + [sibling(one) for one in c_moved]
    if rounds:
        passed, across = over_tensor(branch_shards[3], 1), over_middle(branch_shards[3])
    cot, *second_parts = kernel_call(
        partial(second_grads_body, tz, dp, packets),
        "second_grads",
        [shape((tokens, width), BF)]
        + [shape((width // dp * len(packet), nd + nf), BF) for packet in packets],
        (after(place, branch_shards[1]), aa),
        [pltpu.SemaphoreType.DMA((2 * tz,))],
        LITTLE,
        c_shards,
    )

    if rounds:
        shard = kernel_call(
            pass_body,
            "branch_relay",
            [shape((rows, width), BF)],
            (after(place, second_parts[0]), branch_shards[2], passed),
            [],
            LITTLE,
        )[0]
        branch_moved = [over_tensor(branch_shards[1], 1), over_tensor(shard, 2)]
        branch_moved += [across]
    else:
        shard = branch_shards[1]
        branch_moved = [over_tensor(branch_shards[r], r) for r in range(1, tz)]
    second_first = first_round(second_parts)
    back_own, back_sib, gg, sums = kernel_call(
        partial(backward_body, tz, chips, sizes),
        "backward",
        [
            shape((length, width), BF),
            shape((length + 16, width), BF),
            shape((tokens, nq + nf), BF),
            shape((8, width), F32),
        ],
        (
            after(place, shard),
            table,
            gains,
            cot,
            w,
            qkv,
            lse,
            dgelu,
            stats,
            x,
        ),
        [
            pltpu.VMEM((5, 8, width), F32),
            pltpu.VMEM((length, nd), F32),
            pltpu.VMEM((length, nd), F32),
            pltpu.VMEM((8, nq + nf), F32),
        ],
        14,
    )
    first_parts = kernel_call(
        partial(first_grads_body, dp, packets, nq),
        "first_grads",
        [shape((width // dp * len(packet), nq + nf), BF) for packet in packets],
        (place, n1, n2, gg),
        [],
        LITTLE,
    )
    branch_moved, second_first, back_sib = together(
        branch_moved, second_first, after(back_sib, first_parts[0])
    )
    if rounds:
        branch_moved[2] = jnp.where(middle, branch_moved[2], jnp.zeros((), BF))
    output = (
        inputs.astype(F32)
        + turn(added([branch_shards[0]] + branch_moved))
        + dense_bias
        + fc2_bias
    ).astype(BF)

    if rounds:
        back_other = sibling(back_sib)
        first_first = first_round(first_parts)
        *back_shards, sums = kernel_call(
            partial(split_body, tz),
            "split_back",
            [shape((rows, width), F32)]
            + [shape((rows, width), BF)] * 3
            + [shape(sums.shape, F32)],
            (place, back_own, back_other, sums),
            [],
            LITTLE,
        )
        passed, across = over_tensor(back_shards[3], 1), over_middle(back_shards[3])
        second_messages = kernel_call(
            messages_body,
            "second_messages",
            [shape(second_parts[4].shape, BF)] * 2,
            (after(place, back_other), second_parts[4], second_parts[5], *second_first),
            [],
            LITTLE,
        )
        second_x, second_y = over_chip(second_messages[0], 1), over_chip(second_messages[1], 2)
        near, shard, first_x, first_y, sums = kernel_call(
            relay_body,
            "second_round",
            [
                shape((rows + 16, width), BF),
                shape((rows + 16, width), BF),
                shape(first_parts[4].shape, BF),
                shape(first_parts[5].shape, BF),
                shape(sums.shape, F32),
            ],
            (
                after(place, across),
                back_shards[1],
                back_shards[2],
                passed,
                first_parts[4],
                first_parts[5],
                *first_first,
                sums,
                *[over_chip(sums, flip) for flip in range(1, chips)],
            ),
            [],
            LITTLE,
        )
        biases = sums
        back_second, back_first = over_tensor(shard, 2), over_tensor(near, 1)
        third = over_tensor(sums, 3)
        first_x, first_y = over_chip(first_x, 1), over_chip(first_y, 2)

        def other_sum(parts, first, second, where):
            return kernel_call(
                other_body,
                "other_sum",
                [shape(parts[1].shape, BF)],
                (where, parts[1], first[1], second),
                [],
                LITTLE,
            )[0]

        second_sib = sibling(
            other_sum(second_parts, second_first, second_y, after(place, first_parts[0]))
        )
        first_sib = sibling(other_sum(first_parts, first_first, first_y, place))
        first_terms = [first_parts[0], first_first[0], first_x]
        second_terms = [second_parts[0], second_first[0], second_x]
        dense_grad, fc2_grad = join(second_terms, second_sib, (nd, nf), 0)
        qkv_grad, fc1_grad = join(first_terms, first_sib, (nq, nf), heads)
        input_grad, sums = kernel_call(
            finish_body,
            "finish_rows",
            [shape((rows, width), F32), shape(sums.shape, F32)],
            (
                place,
                back_shards[0],
                back_first,
                back_second,
                across,
                own_rows,
                masked,
                sums,
                third,
            ),
            [],
            6,
        )
    else:
        back_other = sibling(back_sib)
        back_shards = add_sibling(place, back_own, back_other)
        back = added([back_shards[0]] + [over_tensor(back_shards[r], r) for r in range(1, tz)])
        sums = added([sums, back_other[length : length + 8], back_other[length + 8 :]])
        if step % 128:
            sums = jnp.concatenate([turn(sums[:5]), sums[5:]], axis=0)
        value = own_rows.astype(F32)
        center = value - jnp.mean(value, axis=1, keepdims=True)
        spread = lax.rsqrt(jnp.mean(center * center, axis=1, keepdims=True) + EPS)
        scaled = center * spread
        input_grad = masked.astype(F32) + spread * (
            back
            - jnp.mean(back, axis=1, keepdims=True)
            - scaled * jnp.mean(back * scaled, axis=1, keepdims=True)
        )
        (second_own, second_other), (first_own, first_other) = (
            chip_sums(second_parts),
            chip_sums(first_parts),
        )
        second_sib, first_sib = sibling(second_other), sibling(first_other)
        flip = 1
        while flip < chips:
            sums = sums + over_chip(sums, flip)
            flip *= 2
        biases = sums
        sums = added([sums] + [over_tensor(sums, r) for r in range(1, tz)])
        dense_grad, fc2_grad = join([second_own], second_sib, (nd, nf), 0)
        qkv_grad, fc1_grad = join([first_own], first_sib, (nq, nf), heads)
    input_grad = turn(input_grad)

    return (
        output,
        input_grad,
        sums[0],
        sums[1],
        sums[2],
        sums[3],
        qkv_grad,
        biases[5, : 2 * nq],
        dense_grad,
        sums[4],
        fc1_grad,
        biases[6, : 2 * nf],
        fc2_grad,
        sums[4],
    )


def solution(mesh):
    return jax.shard_map(
        partial(on_device, mesh.shape["dp"], mesh.shape["tensor"]),
        mesh=mesh,
        in_specs=(
            P(("dp", "tensor"), None),
            P("dp"),
            P(),
            P(),
            P(),
            P(),
            P("dp", "tensor"),
            P("tensor"),
            P("dp", "tensor"),
            P(),
            P("dp", "tensor"),
            P("tensor"),
            P("dp", "tensor"),
            P(),
            P(("dp", "tensor"), None),
        ),
        out_specs=(
            P(("dp", "tensor"), None),
            P(("dp", "tensor"), None),
            P(),
            P(),
            P(),
            P(),
            P("dp", "tensor"),
            P("tensor"),
            P("dp", "tensor"),
            P(),
            P("dp", "tensor"),
            P("tensor"),
            P("dp", "tensor"),
            P(),
        ),
        check_vma=False,
    )
```

```python
from functools import partial

import jax
import jax.numpy as jnp
from jax import lax
from jax.experimental import pallas as pl
from jax.experimental.pallas import tpu as pltpu
from jax.sharding import PartitionSpec as P

HD = 64
ROT = 16
EPS = 1e-05
SCALE = HD**-0.5
BF = jnp.bfloat16
F32 = jnp.float32
LN_ROWS = 128
ANY = pl.BlockSpec(memory_space=pl.ANY)
HBM = pl.BlockSpec(memory_space=pltpu.HBM)
VMEM = pl.BlockSpec(memory_space=pltpu.VMEM)
SMEM = pl.BlockSpec(memory_space=pltpu.SMEM)
VMEM_LIMIT = 16 * 1024 * 1024
PEAK = 1.15e9
LITTLE = 0.01


def dot(a, b):
    return jnp.dot(a, b, preferred_element_type=F32)


def dot_nt(a, b):
    return lax.dot_general(a, b, (((1,), (1,)), ((), ())), preferred_element_type=F32)


def dot_tn(a, b):
    return lax.dot_general(a, b, (((0,), (0,)), ((), ())), preferred_element_type=F32)


def shape(dims, dtype):
    return jax.ShapeDtypeStruct(dims, dtype)


def kernel_call(body, name, outs, operands, scratch, micros, fetched=(), placed=False):
    return pl.pallas_call(
        body,
        name=name,
        out_shape=outs,
        in_specs=[SMEM] + [VMEM] * (len(operands) - 1) + [HBM] * len(fetched),
        out_specs=[ANY if placed else VMEM] * len(outs),
        scratch_shapes=scratch,
        cost_estimate=pl.CostEstimate(
            flops=int(micros * PEAK), bytes_accessed=0, transcendentals=0
        ),
        compiler_params=pltpu.CompilerParams(vmem_limit_bytes=VMEM_LIMIT),
    )(*operands, *fetched)


def start_all(pairs, sems, first=0):
    copies = [
        pltpu.make_async_copy(src, dst, sems.at[first + i]) for i, (src, dst) in enumerate(pairs)
    ]
    for one in copies:
        one.start()
    return copies


def wait_all(copies):
    for one in copies:
        one.wait()


def rows_at(start, size):
    return pl.ds(pl.multiple_of(start, size), size)


def shard_rows(place, tz, rows, i):
    return i // tz * tz * rows + (place[1] ^ (i % tz)) * rows


def weight_rows(place, size, i):
    return (i - i % 2 + (place[0] ^ (i % 2))) * size


def rotated(values, cos_table, sine_table):
    lane = lax.broadcasted_iota(jnp.int32, values.shape, 1)
    lanes = values.shape[1]
    turned = jnp.where(
        lane % ROT < ROT // 2,
        pltpu.roll(values, lanes - ROT // 2, 1),
        pltpu.roll(values, ROT // 2, 1),
    )
    return values * cos_table + turned * sine_table


def head_mask(value, head, heads):
    lane = lax.broadcasted_iota(jnp.int32, value.shape, 1)
    return (lane // (value.shape[1] // heads)) == head


def allowed_block(first_row, rows, keys, lower):
    row = lax.broadcasted_iota(jnp.int32, (rows, keys), 0) + first_row
    col = lax.broadcasted_iota(jnp.int32, (rows, keys), 1)
    return (col <= row) & (col >= lower)


def store_shards(place, tz, outs, group, cols, value):
    rows = value.shape[0] // tz
    for b in range(tz):
        outs[group][rows_at((place[1] ^ b) * rows, rows), cols] = value[
            b * rows : (b + 1) * rows
        ].astype(BF)


def forward_body(tz, dp, count, sizes, *refs):
    length, width, nq, nf, nd = sizes
    heads = nd // HD
    place, table, gains, shift_qkv, shift_fc1 = refs[:5]
    at = 5
    shards, pieces_w = refs[at : at + 2 * tz], refs[at + 2 * tz : at + 2 * tz + count]
    at += 2 * tz + count
    out_own, out_sib, x, w, n1, n2, qkv, lse, aa, dgelu, stats = refs[at : at + 11]
    x_sems, w_sems = refs[at + 11 :]
    rows = length // tz
    size = width // dp
    x_in = start_all(
        [
            (one, x.at[rows_at(shard_rows(place, tz, rows, i), rows)])
            for i, one in enumerate(shards)
        ],
        x_sems,
    )
    parts_w = [
        one.at[j * size : (j + 1) * size] for one in pieces_w for j in range(one.shape[0] // size)
    ]
    w_in = start_all(
        [(one, w.at[rows_at(weight_rows(place, size, i), size)]) for i, one in enumerate(parts_w)],
        w_sems,
    )
    for i in range(2 * tz):
        x_in[i].wait()
        start = shard_rows(place, tz, rows, i)

        for j in range(rows // LN_ROWS):
            there = rows_at(start + j * LN_ROWS, LN_ROWS)
            value = x[there, :].astype(F32)
            mean = jnp.mean(value, axis=1, keepdims=True)
            center = value - mean
            spread = lax.rsqrt(jnp.mean(center * center, axis=1, keepdims=True) + EPS)
            scaled = center * spread
            n1[there, :] = (scaled * gains[0:1, :] + gains[1:2, :]).astype(BF)
            n2[there, :] = (scaled * gains[2:3, :] + gains[3:4, :]).astype(BF)
            lane = lax.broadcasted_iota(jnp.int32, (LN_ROWS, 128), 1)
            stats[there, :] = jnp.where(lane == 0, mean, spread)
    wait_all(w_in)
    for g in range(2):
        group = slice(g * length, (g + 1) * length)
        cos_table, sine_table = table[group, 0:nd], table[group, nd : 2 * nd]
        projected = dot(n1[group, :], w[:, 0:nq]) + shift_qkv[...]
        qkv[group, 0:nd] = rotated(projected[:, 0:nd], cos_table, sine_table).astype(BF)
        qkv[group, nd : 2 * nd] = rotated(projected[:, nd : 2 * nd], cos_table, sine_table).astype(
            BF
        )
        qkv[group, 2 * nd : 3 * nd] = projected[:, 2 * nd : 3 * nd].astype(BF)
        for part in range(2):
            cols = slice(part * nf // 2, (part + 1) * nf // 2)
            h = dot(n2[group, :], w[:, nq + cols.start : nq + cols.stop]) + shift_fc1[:, cols]
            phi = 0.5 * (1.0 + lax.erf(h * 0.7071067811865476))
            aa[group, nd + cols.start : nd + cols.stop] = (h * phi).astype(BF)
            dgelu[group, cols] = (phi + h * (0.3989422804014327 * jnp.exp(-0.5 * h * h))).astype(BF)

        half = length // 2
        for block in range(2):
            keys = (block + 1) * half
            q_rows = slice(g * length + block * half, g * length + (block + 1) * half)
            k_rows = slice(g * length, g * length + keys)
            q = qkv[q_rows, 0:nd] * SCALE
            k = qkv[k_rows, nd : 2 * nd]
            v = qkv[k_rows, 2 * nd : 3 * nd]
            lower = table[q_rows, 2 * nd : 2 * nd + 1].astype(jnp.int32)
            allowed = allowed_block(block * half, half, keys, lower)
            gathered = jnp.zeros((half, nd), F32)
            kept = jnp.zeros((half, 128), F32)
            lane = lax.broadcasted_iota(jnp.int32, (half, 128), 1)
            for h in range(heads):
                mine = head_mask(q, h, heads)
                scores = dot_nt(jnp.where(mine, q, jnp.zeros_like(q)), k)
                scores = jnp.where(allowed, scores, -jnp.inf)
                top = jnp.max(scores, axis=1, keepdims=True)
                raised = jnp.exp(scores - top)
                total = jnp.sum(raised, axis=1, keepdims=True)
                soft = (raised * (1.0 / total)).astype(BF)
                gathered = jnp.where(mine, dot(soft, v), gathered)
                kept = jnp.where(lane == h, top + jnp.log(total), kept)
            valid = table[q_rows, 2 * nd + 64 : 2 * nd + 65]
            aa[q_rows, 0:nd] = (gathered * valid).astype(BF)
            lse[q_rows, :] = kept

        quarter = width // 4
        for part in range(4):
            cols = slice(part * quarter, (part + 1) * quarter)
            value = dot_nt(aa[group, :], w[cols, nq + nf :])
            store_shards(place, tz, (out_own, out_sib), g, cols, value)


def second_grads_body(tz, dp, packets, place, aa, *refs):
    shards, cot, outs, sems = refs[: 2 * tz], refs[2 * tz], refs[2 * tz + 1 : -1], refs[-1]
    rows = shards[0].shape[0]
    wait_all(
        start_all(
            [
                (one, cot.at[rows_at(shard_rows(place, tz, rows, i), rows)])
                for i, one in enumerate(shards)
            ],
            sems,
        )
    )
    grads_out(dp, packets, place, outs, lambda cols: dot_tn(cot[:, cols], aa[...]))


def first_grads_body(dp, packets, nq, place, n1, n2, gg, *outs):
    grads_out(
        dp,
        packets,
        place,
        outs,
        lambda cols: jnp.concatenate(
            [dot_tn(n1[:, cols], gg[:, 0:nq]), dot_tn(n2[:, cols], gg[:, nq:])], axis=1
        ),
    )


def grads_out(dp, packets, place, outs, product):
    size = outs[0].shape[0]
    slots = {i: (out, slot) for out, packet in zip(outs, packets) for slot, i in enumerate(packet)}
    for r in range(dp // 2):
        value = product(slice(2 * r * size, (2 * r + 2) * size)).astype(BF)
        low, high = value[0:size], value[size : 2 * size]
        first = place[0] == 0
        for i, (one, two) in ((2 * r, (low, high)), (2 * r + 1, (high, low))):
            out, slot = slots[i]
            out[slot * size : (slot + 1) * size, :] = jnp.where(first, one, two)


def eight_rows(value):
    rows, columns = value.shape
    return jnp.sum(value.reshape(rows // 8, 8, columns), axis=0)


def backward_body(tz, chips, sizes, *refs):
    length, width, nq, nf, nd = sizes
    heads = nd // HD
    place, table, gains, cot, w, qkv, lse, dgelu, stats, x = refs[:10]
    out_own, out_sib, gg, sums = refs[10:14]
    acc, dk, dv, bias_sums = refs[14:]
    rows = length // tz
    acc[...] = jnp.zeros_like(acc)
    bias_sums[...] = jnp.zeros_like(bias_sums)
    for g in range(2):
        group = slice(g * length, (g + 1) * length)
        grad_out = dot(cot[group, :], w[:, nq + nf : nq + nf + nd]).astype(BF)
        for part in range(2):
            cols = slice(part * nf // 2, (part + 1) * nf // 2)
            value = dot(cot[group, :], w[:, nq + nf + nd + cols.start : nq + nf + nd + cols.stop])
            value = value * dgelu[group, cols].astype(F32)
            gg[group, nq + cols.start : nq + cols.stop] = value.astype(BF)
            bias_sums[:, nq + cols.start : nq + cols.stop] += eight_rows(value)

        half = length // 2
        dk[...] = jnp.zeros_like(dk)
        dv[...] = jnp.zeros_like(dv)
        for block in range(2):
            keys = (block + 1) * half
            q_rows = slice(g * length + block * half, g * length + (block + 1) * half)
            k_rows = slice(g * length, g * length + keys)
            q = qkv[q_rows, 0:nd] * SCALE
            k = qkv[k_rows, nd : 2 * nd]
            v = qkv[k_rows, 2 * nd : 3 * nd]
            k_scaled = k * SCALE
            go = grad_out[block * half : (block + 1) * half]
            lower = table[q_rows, 2 * nd : 2 * nd + 1].astype(jnp.int32)
            allowed = allowed_block(block * half, half, keys, lower)
            dq = jnp.zeros((half, nd), F32)
            for h in range(heads):
                mine = head_mask(q, h, heads)
                zero = jnp.zeros_like(q)
                q_h = jnp.where(mine, q, zero)
                go_h = jnp.where(mine, go, zero)
                scores = dot_nt(q_h, k)
                probs = jnp.exp(jnp.where(allowed, scores - lse[q_rows, h : h + 1], -jnp.inf))
                grad_soft = dot_nt(go_h, v)
                inner = jnp.sum(probs * grad_soft, axis=1, keepdims=True)
                grad_scores = (probs * (grad_soft - inner)).astype(BF)
                dq = jnp.where(mine, dot(grad_scores, k_scaled), dq)
                dk[0:keys, :] += dot_tn(grad_scores, q_h)
                dv[0:keys, :] += dot_tn(probs.astype(BF), go_h)
            grads_q = rotated(dq, table[q_rows, 0:nd], -table[q_rows, nd : 2 * nd])
            gg[q_rows, 0:nd] = grads_q.astype(BF)
            bias_sums[:, 0:nd] += eight_rows(grads_q)
        grads_k = rotated(dk[...], table[group, 0:nd], -table[group, nd : 2 * nd])
        gg[group, nd : 2 * nd] = grads_k.astype(BF)
        gg[group, 2 * nd : 3 * nd] = dv[...].astype(BF)
        bias_sums[:, nd : 2 * nd] += eight_rows(grads_k)
        bias_sums[:, 2 * nd : 3 * nd] += eight_rows(dv[...])

        mean, spread = stats[group, 0:1], stats[group, 1:2]
        quarter = width // 4
        for part in range(4):
            cols = slice(part * quarter, (part + 1) * quarter)
            one = dot_nt(gg[group, 0:nq], w[cols, 0:nq])
            two = dot_nt(gg[group, nq:], w[cols, nq : nq + nf])
            scaled = (x[group, cols].astype(F32) - mean) * spread
            for slot, value in enumerate((one * scaled, one, two * scaled, two)):
                acc[slot, :, cols] += eight_rows(value)
            value = one * gains[0:1, cols] + two * gains[2:3, cols]
            store_shards(place, tz, (out_own, out_sib), g, cols, value)
    sums[...] = jnp.zeros_like(sums)
    own = cot[rows_at(place[1] * rows, rows), :].astype(F32)
    acc[4] = eight_rows(own)
    step = width // chips
    for i in range(5):
        total = jnp.sum(acc[i], axis=0, keepdims=True)
        if step % 128 == 0:
            for r in range(chips):
                at = pl.ds(pl.multiple_of((place[3] ^ r) * step, step), step)
                sums[i : i + 1, at] = total[:, r * step : (r + 1) * step]
        else:
            sums[i : i + 1, :] = total
    total = jnp.sum(bias_sums[...], axis=0, keepdims=True)
    sums[5:6, pl.ds(pl.multiple_of(place[0] * nq, nq), nq)] = by_head(total[:, :nq], heads)
    sums[6:7, pl.ds(pl.multiple_of(place[0] * nf, nf), nf)] = total[:, nq:]
    put_sums(out_sib, length, sums[...])


def put_sums(out, row, value):
    high = value.astype(BF).astype(F32)
    out[row : row + 16, :] = jnp.concatenate([high, value - high], axis=0).astype(BF)


def get_sums(ref, row):
    return ref[row : row + 8, :].astype(F32) + ref[row + 8 : row + 16, :].astype(F32)


def combine_body(tz, place, own, other, *outs):
    rows = own.shape[0] // tz
    for r, out in enumerate(outs):
        at = slice(r * rows, (r + 1) * rows)
        out[0:rows, :] = (own[at, :].astype(F32) + other[at, :].astype(F32)).astype(out.dtype)


def by_kind(values, heads):
    parts = [
        values[..., (h * 3 + kind) * HD : (h * 3 + kind + 1) * HD]
        for kind in range(3)
        for h in range(heads)
    ]
    return jnp.concatenate(parts, axis=-1)


def by_head(values, heads):
    parts = [
        values[..., (kind * heads + h) * HD : (kind * heads + h + 1) * HD]
        for h in range(heads)
        for kind in range(3)
    ]
    return jnp.concatenate(parts, axis=-1)


def pack_body(sizes, place, qkv_in, fc1_in, dense_in, fc2_in, kept, given, *scratch):
    nq, nf, nd = sizes
    qkv, fc1, dense, fc2, sems = scratch
    wait_all(
        start_all([(qkv_in, qkv), (fc1_in, fc1), (dense_in, dense), (fc2_in, fc2)], sems)
    )
    for out, which in ((given, 1 - place[0]), (kept, place[0])):

        def half(ref, size):
            return ref[:, pl.ds(pl.multiple_of(which * size, size), size)]

        out[:, 0:nq] = by_kind(half(qkv, nq), nd // HD)
        out[:, nq : nq + nf] = half(fc1, nf)
        out[:, nq + nf : nq + nf + nd] = half(dense, nd)
        out[:, nq + nf + nd :] = half(fc2, nf)


def split_body(tz, place, own, other, *refs):
    sums, outs = refs[: -tz - 1], refs[-tz - 1 :]
    combine_body(tz, place, own, other, *outs[:tz])
    add_sums(sums, outs[tz])


def add_sums(refs, out):
    total = refs[0][...]
    for one in refs[1:]:
        total = total + one[...]
    out[...] = total


def pass_body(place, shard, passed, out):
    rows = shard.shape[0]
    keep = (place[2] == 1).astype(F32)
    out[0:rows, :] = (shard[...].astype(F32) + keep * passed[...].astype(F32)).astype(BF)


def relay_body(place, near, shard, passed, *refs):
    first, second, sums = refs[:4], refs[4:8], refs[8:-5]
    out_near, out_shard, out_x, out_y, out_sums = refs[-5:]
    rows = near.shape[0]
    add_sums(sums, out_sums)
    total = out_sums[...]
    out_near[0:rows, :] = near[...]
    pass_body(place, shard, passed, out_shard)
    for out in (out_near, out_shard):
        put_sums(out, rows, total)
    at = 0
    for to_x, to_y, from_y, from_x in (first, second):
        size, columns = to_x.shape
        cols = slice(at, at + columns)
        out_x[:, cols] = to_x[...] + from_y[size : 2 * size, :]
        out_y[:, cols] = to_y[...] + from_x[size : 2 * size, :]
        at += columns


def other_body(place, first, first_x, second, second_x, from_y, out):
    size, at = out.shape[0], 0
    for mine, from_x in ((first, first_x), (second, second_x)):
        cols = slice(at, at + mine.shape[1])
        out[:, cols] = (
            mine[...].astype(F32) + from_x[0:size, :].astype(F32) + from_y[:, cols].astype(F32)
        ).astype(BF)
        at += mine.shape[1]


def finish_body(place, own, first, second, across, x, cot, sums, third, out_rows, out_sums):
    rows = own.shape[0]
    keep = (place[2] == 1).astype(F32)
    back = (
        own[...]
        + first[0:rows, :].astype(F32)
        + second[0:rows, :].astype(F32)
        + keep * across[...].astype(F32)
    )
    value = x[...].astype(F32)
    center = value - jnp.mean(value, axis=1, keepdims=True)
    spread = lax.rsqrt(jnp.mean(center * center, axis=1, keepdims=True) + EPS)
    scaled = center * spread
    out_rows[...] = cot[...].astype(F32) + spread * (
        back
        - jnp.mean(back, axis=1, keepdims=True)
        - scaled * jnp.mean(back * scaled, axis=1, keepdims=True)
    )
    out_sums[...] = sums[...] + get_sums(first, rows) + get_sums(second, rows) + third[...]


def join_body(heads, widths, count, place, *refs):
    parts, other, outs = refs[:count], refs[count], refs[count + 1 :]
    rows = other.shape[0]
    sums, at = [], 0
    while at < count:
        total, columns = parts[at][0:rows, :].astype(F32), parts[at].shape[1]
        at += 1
        while at < count and parts[at].shape[1] == columns:
            total = total + parts[at][0:rows, :].astype(F32)
            at += 1
        sums.append(total)
    if len(sums) == 3:
        sums = [jnp.concatenate(sums[:2], axis=1) + sums[2]]
    for half, which in ((sums[0], place[0]), (other[...].astype(F32), 1 - place[0])):
        at = 0
        for i, (out, size) in enumerate(zip(outs, widths)):
            value = half[:, at : at + size]
            if i == 0 and heads:
                value = by_head(value, heads)
            out[:, pl.ds(pl.multiple_of(which * size, size), size)] = value
            at += size


def xor_pairs(size, flip):
    return [(i, i ^ flip) for i in range(size)]


def on_device(
    dp,
    tz,
    inputs,
    segment_ids,
    ln1_gain,
    ln1_bias,
    ln2_gain,
    ln2_bias,
    qkv_weight,
    qkv_bias,
    dense_weight,
    dense_bias,
    fc1_weight,
    fc1_bias,
    fc2_weight,
    fc2_bias,
    cotangent,
):
    rows, width = inputs.shape
    length = segment_ids.shape[0]
    tokens = 2 * length
    chips = dp // 2
    here = lax.axis_index("dp")
    core = here % 2
    chip = here // 2
    tensor = lax.axis_index("tensor")
    step = width // chips
    nq, nf, nd = qkv_weight.shape[1] // 2, fc1_weight.shape[1] // 2, dense_weight.shape[1] // 2
    wide = nq + nf + nd + nf
    heads = nd // HD
    sizes = (length, width, nq, nf, nd)
    middle = (tensor == 1) | (tensor == 2)
    place = jnp.stack([core, tensor, middle, chip]).astype(jnp.int32)

    def turn(values):
        parts = [
            lax.dynamic_slice_in_dim(values, (chip ^ r) * step, step, axis=values.ndim - 1)
            for r in range(chips)
        ]
        return jnp.concatenate(parts, axis=-1)

    def sibling(values):
        return lax.ppermute(values, "dp", xor_pairs(dp, 1))

    def over_chip(values, flip):
        return lax.ppermute(values, "dp", xor_pairs(dp, 2 * flip))

    def over_tensor(values, flip):
        return lax.ppermute(values, "tensor", xor_pairs(tz, flip))

    def together(*values):
        return lax.optimization_barrier(values)

    def after(values, event):
        return lax.optimization_barrier((values, event))[0]

    def over_middle(values):
        return lax.ppermute(values, "tensor", [(0, 0), (1, 2), (2, 1), (3, 3)])

    def add_sibling(place, own, other):
        dtypes = [F32] + [BF] * (tz - 1)
        return kernel_call(
            partial(combine_body, tz),
            "add_sibling",
            [shape((rows, width), d) for d in dtypes],
            (place, own, other),
            [],
            LITTLE,
        )

    def added(parts):
        total = parts[0]
        for one in parts[1:]:
            total = total + one.astype(F32)
        return total

    def row_tables(arrived):
        both_ids = jnp.stack([segment_ids, sibling(after(segment_ids, arrived))])
        earlier = (both_ids[:, None, :] >= 0) & (both_ids[:, None, :] < both_ids[:, :, None])
        begins = jnp.sum(earlier.astype(jnp.int32), axis=2).reshape(tokens)
        flat_ids = both_ids.reshape(tokens)
        index = jnp.arange(tokens, dtype=jnp.int32) % length
        position = (index - begins).astype(F32)
        lane = jnp.arange(nd, dtype=jnp.int32) % HD
        half_rot = ROT // 2
        frequency = jnp.where(
            lane < ROT, 10000.0 ** (-2.0 * (lane % half_rot).astype(F32) / ROT), 0.0
        )
        angles = position[:, None] * frequency[None, :]
        sign = jnp.where(lane < half_rot, -1.0, 1.0)
        lower = jnp.where(flat_ids >= 0, begins, index).astype(F32)
        valid = (flat_ids >= 0).astype(F32)
        last = jnp.where(jnp.arange(128)[None, :] < 64, lower[:, None], valid[:, None])
        return jnp.concatenate([jnp.cos(angles), jnp.sin(angles) * sign, last], axis=1)

    def gather(kept, given, own_rows, later):
        if chips != 4 or tz != 4:
            blocks = [(kept, sibling(given))]
            flip = 1
            while flip < chips:
                blocks = blocks + [(over_chip(a, flip), over_chip(b, flip)) for a, b in blocks]
                flip *= 2
            shards = [own_rows] + [over_tensor(own_rows, r) for r in range(1, tz)]
            return (
                [one for block in blocks for one in block],
                shards + [sibling(one) for one in shards],
                later,
                row_tables(given),
            )
        moved = [over_tensor(own_rows, r) for r in range(1, tz)]
        kept_x, kept_y, given = together(over_chip(kept, 1), over_chip(kept, 2), sibling(given))
        table = row_tables(kept_x)
        given_x, given_y = over_chip(given, 1), over_chip(given, 2)
        moved, kept_x, given_x, given_y, table = together(moved, kept_x, given_x, given_y, table)
        later = after(later, moved)
        pieces = [kept, given, kept_x, given_x, kept_y, given_y]
        pieces += [over_chip(kept_x, 2), over_chip(given_y, 1)]
        shards = [own_rows] + moved
        return pieces, shards + [sibling(one) for one in shards], later, table

    rounds = chips == 4 and tz == 4
    packets = [[0], [1], [4, 6], [3, 7], [2], [5]] if rounds else [[i] for i in range(dp)]

    def first_round(parts):
        if rounds:
            return [over_chip(parts[2], 2), over_chip(parts[3], 1)]
        return []

    def chip_sums(parts):
        blocks = [(parts[2 * r], parts[2 * r + 1]) for r in range(chips)]
        flip = chips // 2
        while flip:
            blocks = [
                tuple(
                    (a.astype(F32) + over_chip(b, flip).astype(F32)).astype(BF)
                    for a, b in zip(blocks[r], blocks[r + flip])
                )
                for r in range(flip)
            ]
            flip //= 2
        return blocks[0]

    def join(terms, other, widths, own_heads):
        return kernel_call(
            partial(join_body, own_heads, widths, len(terms)),
            "join_halves",
            [shape((width // dp, 2 * one), F32) for one in widths],
            (place, *terms, other),
            [],
            LITTLE,
        )

    def half_of(values, which):
        size = values.shape[-1] // 2
        return lax.dynamic_slice_in_dim(values, which * size, size, axis=values.ndim - 1)


    kept, given = kernel_call(
        partial(pack_body, (nq, nf, nd)),
        "pack_weights",
        [shape((width // dp, wide), BF)] * 2,
        (place,),
        [
            pltpu.VMEM(one.shape, BF) for one in (qkv_weight, fc1_weight, dense_weight, fc2_weight)
        ]
        + [pltpu.SemaphoreType.DMA((4,))],
        LITTLE,
        [
            pltpu.with_memory_space_constraint(one, pltpu.HBM)
            for one in (qkv_weight, fc1_weight, dense_weight, fc2_weight)
        ],
    )

    own_rows = turn(after(inputs, kept))
    own_validity = lax.dynamic_slice_in_dim(segment_ids, tensor * rows, rows) >= 0
    masked = jnp.where(own_validity[:, None], turn(cotangent), jnp.zeros((), BF))
    weights, x_shards, masked, table = gather(kept, given, own_rows, masked)
    c_moved = [over_tensor(masked, r) for r in range(1, tz)]
    masked_sib = sibling(masked)

    gains = turn(jnp.stack([ln1_gain, ln1_bias, ln2_gain, ln2_bias]))
    shift_qkv = by_kind(half_of(qkv_bias, core), heads)[None, :]
    shift_fc1 = half_of(fc1_bias, core)[None, :]

    part_own, part_sib, x, w, n1, n2, qkv, lse, aa, dgelu, stats = kernel_call(
        partial(forward_body, tz, dp, len(weights), sizes),
        "forward",
        [
            shape((length, width), BF),
            shape((length, width), BF),
            shape((tokens, width), BF),
            shape((width, wide), BF),
            shape((tokens, width), BF),
            shape((tokens, width), BF),
            shape((tokens, nq), BF),
            shape((tokens, 128), F32),
            shape((tokens, nd + nf), BF),
            shape((tokens, nf), BF),
            shape((tokens, 128), F32),
        ],
        (after(place, masked_sib), table, gains, shift_qkv, shift_fc1),
        [pltpu.SemaphoreType.DMA((2 * tz,)), pltpu.SemaphoreType.DMA((dp,))],
        LITTLE,
        (*x_shards, *weights),
    )

    c_moved, part_sib = together(c_moved, part_sib)
    part_other = sibling(part_sib)
    branch_shards = add_sibling(place, part_own, part_other)
    c_shards = [masked] + c_moved + [masked_sib]
    c_shards += [sibling(one) for one in after(c_moved, part_other)]
    if rounds:
        passed, across = over_tensor(branch_shards[3], 1), over_middle(branch_shards[3])
    cot, *second_parts = kernel_call(
        partial(second_grads_body, tz, dp, packets),
        "second_grads",
        [shape((tokens, width), BF)]
        + [shape((width // dp * len(packet), nd + nf), BF) for packet in packets],
        (after(place, branch_shards[1]), aa),
        [pltpu.SemaphoreType.DMA((2 * tz,))],
        LITTLE,
        c_shards,
    )

    if rounds:
        shard = kernel_call(
            pass_body,
            "branch_relay",
            [shape((rows, width), BF)],
            (after(place, second_parts[0]), branch_shards[2], passed),
            [],
            LITTLE,
        )[0]
        branch_moved = [over_tensor(branch_shards[1], 1), over_tensor(shard, 2)]
        branch_moved += [across]
    else:
        shard = branch_shards[1]
        branch_moved = [over_tensor(branch_shards[r], r) for r in range(1, tz)]
    second_first = first_round(second_parts)
    back_own, back_sib, gg, sums = kernel_call(
        partial(backward_body, tz, chips, sizes),
        "backward",
        [
            shape((length, width), BF),
            shape((length + 16, width), BF),
            shape((tokens, nq + nf), BF),
            shape((8, width), F32),
        ],
        (
            after(place, shard),
            table,
            gains,
            cot,
            w,
            qkv,
            lse,
            dgelu,
            stats,
            x,
        ),
        [
            pltpu.VMEM((5, 8, width), F32),
            pltpu.VMEM((length, nd), F32),
            pltpu.VMEM((length, nd), F32),
            pltpu.VMEM((8, nq + nf), F32),
        ],
        14,
    )
    first_parts = kernel_call(
        partial(first_grads_body, dp, packets, nq),
        "first_grads",
        [shape((width // dp * len(packet), nq + nf), BF) for packet in packets],
        (place, n1, n2, gg),
        [],
        LITTLE,
    )
    branch_moved, second_first, back_sib = together(
        branch_moved, second_first, after(back_sib, first_parts[0])
    )
    if rounds:
        branch_moved[2] = jnp.where(middle, branch_moved[2], jnp.zeros((), BF))
    output = (
        inputs.astype(F32)
        + turn(added([branch_shards[0]] + branch_moved))
        + dense_bias
        + fc2_bias
    ).astype(BF)

    if rounds:
        back_other = sibling(back_sib)
        first_parts = list(first_parts)
        sums_chips = [over_chip(sums, flip) for flip in range(1, chips)]
        first_parts[2], first_parts[3], sums_chips = together(
            first_parts[2], first_parts[3], sums_chips
        )
        first_first = first_round(first_parts)
        *back_shards, sums = kernel_call(
            partial(split_body, tz),
            "split_back",
            [shape((rows, width), F32)]
            + [shape((rows, width), BF)] * 3
            + [shape(sums.shape, F32)],
            (place, back_own, back_other, sums, *sums_chips),
            [],
            LITTLE,
        )
        passed, across = over_tensor(back_shards[3], 1), over_middle(back_shards[3])
        near, shard, from_x, from_y, sums = kernel_call(
            relay_body,
            "second_round",
            [
                shape((rows + 16, width), BF),
                shape((rows + 16, width), BF),
                shape((width // dp, wide), BF),
                shape((width // dp, wide), BF),
                shape(sums.shape, F32),
            ],
            (
                after(place, across),
                back_shards[1],
                back_shards[2],
                passed,
                first_parts[4],
                first_parts[5],
                *first_first,
                second_parts[4],
                second_parts[5],
                *second_first,
                sums,
                sibling(sums),
            ),
            [],
            LITTLE,
        )
        biases = sums
        back_second, back_first = over_tensor(shard, 2), over_tensor(near, 1)
        third = over_tensor(sums, 3)
        from_x, from_y = over_chip(from_x, 1), over_chip(from_y, 2)
        other = kernel_call(
            other_body,
            "other_sums",
            [shape((width // dp, wide), BF)],
            (place, first_parts[1], first_first[1], second_parts[1], second_first[1], from_y),
            [],
            LITTLE,
        )[0]
        own_parts = [first_parts[0], first_first[0], second_parts[0], second_first[0], from_x]
        qkv_grad, fc1_grad, dense_grad, fc2_grad = join(
            own_parts, sibling(other), (nq, nf, nd, nf), heads
        )
        input_grad, sums = kernel_call(
            finish_body,
            "finish_rows",
            [shape((rows, width), F32), shape(sums.shape, F32)],
            (
                after(place, other),
                back_shards[0],
                back_first,
                back_second,
                across,
                own_rows,
                masked,
                sums,
                third,
            ),
            [],
            6,
        )
    else:
        back_other = sibling(back_sib)
        back_shards = add_sibling(place, back_own, back_other)
        back = added([back_shards[0]] + [over_tensor(back_shards[r], r) for r in range(1, tz)])
        sums = added([sums, back_other[length : length + 8], back_other[length + 8 :]])
        if step % 128:
            sums = jnp.concatenate([turn(sums[:5]), sums[5:]], axis=0)
        value = own_rows.astype(F32)
        center = value - jnp.mean(value, axis=1, keepdims=True)
        spread = lax.rsqrt(jnp.mean(center * center, axis=1, keepdims=True) + EPS)
        scaled = center * spread
        input_grad = masked.astype(F32) + spread * (
            back
            - jnp.mean(back, axis=1, keepdims=True)
            - scaled * jnp.mean(back * scaled, axis=1, keepdims=True)
        )
        (second_own, second_other), (first_own, first_other) = (
            chip_sums(second_parts),
            chip_sums(first_parts),
        )
        second_sib, first_sib = sibling(second_other), sibling(first_other)
        flip = 1
        while flip < chips:
            sums = sums + over_chip(sums, flip)
            flip *= 2
        biases = sums
        sums = added([sums] + [over_tensor(sums, r) for r in range(1, tz)])
        dense_grad, fc2_grad = join([second_own], second_sib, (nd, nf), 0)
        qkv_grad, fc1_grad = join([first_own], first_sib, (nq, nf), heads)
    input_grad = turn(input_grad)

    return (
        output,
        input_grad,
        sums[0],
        sums[1],
        sums[2],
        sums[3],
        qkv_grad,
        biases[5, : 2 * nq],
        dense_grad,
        sums[4],
        fc1_grad,
        biases[6, : 2 * nf],
        fc2_grad,
        sums[4],
    )


def solution(mesh):
    return jax.shard_map(
        partial(on_device, mesh.shape["dp"], mesh.shape["tensor"]),
        mesh=mesh,
        in_specs=(
            P(("dp", "tensor"), None),
            P("dp"),
            P(),
            P(),
            P(),
            P(),
            P("dp", "tensor"),
            P("tensor"),
            P("dp", "tensor"),
            P(),
            P("dp", "tensor"),
            P("tensor"),
            P("dp", "tensor"),
            P(),
            P(("dp", "tensor"), None),
        ),
        out_specs=(
            P(("dp", "tensor"), None),
            P(("dp", "tensor"), None),
            P(),
            P(),
            P(),
            P(),
            P("dp", "tensor"),
            P("tensor"),
            P("dp", "tensor"),
            P(),
            P("dp", "tensor"),
            P("tensor"),
            P("dp", "tensor"),
            P(),
        ),
        check_vma=False,
    )
```

```python
from functools import partial

import jax
import jax.numpy as jnp
from jax import lax
from jax.experimental import pallas as pl
from jax.experimental.pallas import tpu as pltpu
from jax.sharding import PartitionSpec as P

HD = 64
ROT = 16
EPS = 1e-05
SCALE = HD**-0.5
BF = jnp.bfloat16
F32 = jnp.float32
LN_ROWS = 128
ANY = pl.BlockSpec(memory_space=pl.ANY)
HBM = pl.BlockSpec(memory_space=pltpu.HBM)
VMEM = pl.BlockSpec(memory_space=pltpu.VMEM)
SMEM = pl.BlockSpec(memory_space=pltpu.SMEM)
VMEM_LIMIT = 16 * 1024 * 1024
PEAK = 1.15e9
LITTLE = 0.01


def dot(a, b):
    return jnp.dot(a, b, preferred_element_type=F32)


def dot_nt(a, b):
    return lax.dot_general(a, b, (((1,), (1,)), ((), ())), preferred_element_type=F32)


def dot_tn(a, b):
    return lax.dot_general(a, b, (((0,), (0,)), ((), ())), preferred_element_type=F32)


def shape(dims, dtype):
    return jax.ShapeDtypeStruct(dims, dtype)


def kernel_call(body, name, outs, operands, scratch, micros, fetched=(), placed=False):
    return pl.pallas_call(
        body,
        name=name,
        out_shape=outs,
        in_specs=[SMEM] + [VMEM] * (len(operands) - 1) + [HBM] * len(fetched),
        out_specs=[ANY if placed else VMEM] * len(outs),
        scratch_shapes=scratch,
        cost_estimate=pl.CostEstimate(
            flops=int(micros * PEAK), bytes_accessed=0, transcendentals=0
        ),
        compiler_params=pltpu.CompilerParams(vmem_limit_bytes=VMEM_LIMIT),
    )(*operands, *fetched)


def start_all(pairs, sems, first=0):
    copies = [
        pltpu.make_async_copy(src, dst, sems.at[first + i]) for i, (src, dst) in enumerate(pairs)
    ]
    for one in copies:
        one.start()
    return copies


def wait_all(copies):
    for one in copies:
        one.wait()


def rows_at(start, size):
    return pl.ds(pl.multiple_of(start, size), size)


def shard_rows(place, tz, rows, i):
    return i // tz * tz * rows + (place[1] ^ (i % tz)) * rows


def weight_rows(place, size, i):
    return (i - i % 2 + (place[0] ^ (i % 2))) * size


def rotated(values, cos_table, sine_table):
    lane = lax.broadcasted_iota(jnp.int32, values.shape, 1)
    lanes = values.shape[1]
    turned = jnp.where(
        lane % ROT < ROT // 2,
        pltpu.roll(values, lanes - ROT // 2, 1),
        pltpu.roll(values, ROT // 2, 1),
    )
    return values * cos_table + turned * sine_table


def head_mask(value, head, heads):
    lane = lax.broadcasted_iota(jnp.int32, value.shape, 1)
    return (lane // (value.shape[1] // heads)) == head


def allowed_block(first_row, rows, keys, lower):
    row = lax.broadcasted_iota(jnp.int32, (rows, keys), 0) + first_row
    col = lax.broadcasted_iota(jnp.int32, (rows, keys), 1)
    return (col <= row) & (col >= lower)


def store_shards(place, tz, outs, group, cols, value):
    rows = value.shape[0] // tz
    for b in range(tz):
        outs[group][rows_at((place[1] ^ b) * rows, rows), cols] = value[
            b * rows : (b + 1) * rows
        ].astype(BF)


def forward_body(tz, dp, count, sizes, *refs):
    length, width, nq, nf, nd = sizes
    heads = nd // HD
    place, table, gains, shift_qkv, shift_fc1 = refs[:5]
    at = 5
    shards, pieces_w = refs[at : at + 2 * tz], refs[at + 2 * tz : at + 2 * tz + count]
    at += 2 * tz + count
    out_own, out_sib, x, w, n1, n2, qkv, lse, aa, dgelu, stats = refs[at : at + 11]
    x_sems, w_sems = refs[at + 11 :]
    rows = length // tz
    size = width // dp
    x_in = start_all(
        [
            (one, x.at[rows_at(shard_rows(place, tz, rows, i), rows)])
            for i, one in enumerate(shards)
        ],
        x_sems,
    )
    parts_w = [
        one.at[j * size : (j + 1) * size] for one in pieces_w for j in range(one.shape[0] // size)
    ]
    w_in = start_all(
        [(one, w.at[rows_at(weight_rows(place, size, i), size)]) for i, one in enumerate(parts_w)],
        w_sems,
    )
    for i in range(2 * tz):
        x_in[i].wait()
        start = shard_rows(place, tz, rows, i)

        for j in range(rows // LN_ROWS):
            there = rows_at(start + j * LN_ROWS, LN_ROWS)
            value = x[there, :].astype(F32)
            mean = jnp.mean(value, axis=1, keepdims=True)
            center = value - mean
            spread = lax.rsqrt(jnp.mean(center * center, axis=1, keepdims=True) + EPS)
            scaled = center * spread
            n1[there, :] = (scaled * gains[0:1, :] + gains[1:2, :]).astype(BF)
            n2[there, :] = (scaled * gains[2:3, :] + gains[3:4, :]).astype(BF)
            lane = lax.broadcasted_iota(jnp.int32, (LN_ROWS, 128), 1)
            stats[there, :] = jnp.where(lane == 0, mean, spread)
    wait_all(w_in)
    for g in range(2):
        group = slice(g * length, (g + 1) * length)
        cos_table, sine_table = table[group, 0:nd], table[group, nd : 2 * nd]
        projected = dot(n1[group, :], w[:, 0:nq]) + shift_qkv[...]
        qkv[group, 0:nd] = rotated(projected[:, 0:nd], cos_table, sine_table).astype(BF)
        qkv[group, nd : 2 * nd] = rotated(projected[:, nd : 2 * nd], cos_table, sine_table).astype(
            BF
        )
        qkv[group, 2 * nd : 3 * nd] = projected[:, 2 * nd : 3 * nd].astype(BF)
        for part in range(2):
            cols = slice(part * nf // 2, (part + 1) * nf // 2)
            h = dot(n2[group, :], w[:, nq + cols.start : nq + cols.stop]) + shift_fc1[:, cols]
            phi = 0.5 * (1.0 + lax.erf(h * 0.7071067811865476))
            aa[group, nd + cols.start : nd + cols.stop] = (h * phi).astype(BF)
            dgelu[group, cols] = (phi + h * (0.3989422804014327 * jnp.exp(-0.5 * h * h))).astype(BF)

        half = length // 2
        for block in range(2):
            keys = (block + 1) * half
            q_rows = slice(g * length + block * half, g * length + (block + 1) * half)
            k_rows = slice(g * length, g * length + keys)
            q = qkv[q_rows, 0:nd] * SCALE
            k = qkv[k_rows, nd : 2 * nd]
            v = qkv[k_rows, 2 * nd : 3 * nd]
            lower = table[q_rows, 2 * nd : 2 * nd + 1].astype(jnp.int32)
            allowed = allowed_block(block * half, half, keys, lower)
            gathered = jnp.zeros((half, nd), F32)
            kept = jnp.zeros((half, 128), F32)
            lane = lax.broadcasted_iota(jnp.int32, (half, 128), 1)
            for h in range(heads):
                mine = head_mask(q, h, heads)
                scores = dot_nt(jnp.where(mine, q, jnp.zeros_like(q)), k)
                scores = jnp.where(allowed, scores, -jnp.inf)
                top = jnp.max(scores, axis=1, keepdims=True)
                raised = jnp.exp(scores - top)
                total = jnp.sum(raised, axis=1, keepdims=True)
                soft = (raised * (1.0 / total)).astype(BF)
                gathered = jnp.where(mine, dot(soft, v), gathered)
                kept = jnp.where(lane == h, top + jnp.log(total), kept)
            valid = table[q_rows, 2 * nd + 64 : 2 * nd + 65]
            aa[q_rows, 0:nd] = (gathered * valid).astype(BF)
            lse[q_rows, :] = kept

        quarter = width // 4
        for part in range(4):
            cols = slice(part * quarter, (part + 1) * quarter)
            value = dot_nt(aa[group, :], w[cols, nq + nf :])
            store_shards(place, tz, (out_own, out_sib), g, cols, value)


def second_grads_body(tz, dp, packets, place, aa, *refs):
    shards, cot, outs, sems = refs[: 2 * tz], refs[2 * tz], refs[2 * tz + 1 : -1], refs[-1]
    rows = shards[0].shape[0]
    wait_all(
        start_all(
            [
                (one, cot.at[rows_at(shard_rows(place, tz, rows, i), rows)])
                for i, one in enumerate(shards)
            ],
            sems,
        )
    )
    grads_out(dp, packets, place, outs, lambda cols: dot_tn(cot[:, cols], aa[...]))


def first_grads_body(dp, packets, nq, place, n1, n2, gg, *outs):
    grads_out(
        dp,
        packets,
        place,
        outs,
        lambda cols: jnp.concatenate(
            [dot_tn(n1[:, cols], gg[:, 0:nq]), dot_tn(n2[:, cols], gg[:, nq:])], axis=1
        ),
    )


def grads_out(dp, packets, place, outs, product):
    size = outs[0].shape[0]
    slots = {i: (out, slot) for out, packet in zip(outs, packets) for slot, i in enumerate(packet)}
    for r in range(dp // 2):
        value = product(slice(2 * r * size, (2 * r + 2) * size)).astype(BF)
        low, high = value[0:size], value[size : 2 * size]
        first = place[0] == 0
        for i, (one, two) in ((2 * r, (low, high)), (2 * r + 1, (high, low))):
            out, slot = slots[i]
            out[slot * size : (slot + 1) * size, :] = jnp.where(first, one, two)


def eight_rows(value):
    rows, columns = value.shape
    return jnp.sum(value.reshape(rows // 8, 8, columns), axis=0)


def backward_body(tz, chips, sizes, *refs):
    length, width, nq, nf, nd = sizes
    heads = nd // HD
    place, table, gains, cot, w, qkv, lse, dgelu, stats, x = refs[:10]
    out_own, out_sib, gg, sums = refs[10:14]
    acc, dk, dv, bias_sums = refs[14:]
    rows = length // tz
    acc[...] = jnp.zeros_like(acc)
    bias_sums[...] = jnp.zeros_like(bias_sums)
    for g in range(2):
        group = slice(g * length, (g + 1) * length)
        grad_out = dot(cot[group, :], w[:, nq + nf : nq + nf + nd]).astype(BF)
        for part in range(2):
            cols = slice(part * nf // 2, (part + 1) * nf // 2)
            value = dot(cot[group, :], w[:, nq + nf + nd + cols.start : nq + nf + nd + cols.stop])
            value = value * dgelu[group, cols].astype(F32)
            gg[group, nq + cols.start : nq + cols.stop] = value.astype(BF)
            bias_sums[:, nq + cols.start : nq + cols.stop] += eight_rows(value)

        half = length // 2
        dk[...] = jnp.zeros_like(dk)
        dv[...] = jnp.zeros_like(dv)
        for block in range(2):
            keys = (block + 1) * half
            q_rows = slice(g * length + block * half, g * length + (block + 1) * half)
            k_rows = slice(g * length, g * length + keys)
            q = qkv[q_rows, 0:nd] * SCALE
            k = qkv[k_rows, nd : 2 * nd]
            v = qkv[k_rows, 2 * nd : 3 * nd]
            k_scaled = k * SCALE
            go = grad_out[block * half : (block + 1) * half]
            lower = table[q_rows, 2 * nd : 2 * nd + 1].astype(jnp.int32)
            allowed = allowed_block(block * half, half, keys, lower)
            dq = jnp.zeros((half, nd), F32)
            for h in range(heads):
                mine = head_mask(q, h, heads)
                zero = jnp.zeros_like(q)
                q_h = jnp.where(mine, q, zero)
                go_h = jnp.where(mine, go, zero)
                scores = dot_nt(q_h, k)
                probs = jnp.exp(jnp.where(allowed, scores - lse[q_rows, h : h + 1], -jnp.inf))
                grad_soft = dot_nt(go_h, v)
                inner = jnp.sum(probs * grad_soft, axis=1, keepdims=True)
                grad_scores = (probs * (grad_soft - inner)).astype(BF)
                dq = jnp.where(mine, dot(grad_scores, k_scaled), dq)
                dk[0:keys, :] += dot_tn(grad_scores, q_h)
                dv[0:keys, :] += dot_tn(probs.astype(BF), go_h)
            grads_q = rotated(dq, table[q_rows, 0:nd], -table[q_rows, nd : 2 * nd])
            gg[q_rows, 0:nd] = grads_q.astype(BF)
            bias_sums[:, 0:nd] += eight_rows(grads_q)
        grads_k = rotated(dk[...], table[group, 0:nd], -table[group, nd : 2 * nd])
        gg[group, nd : 2 * nd] = grads_k.astype(BF)
        gg[group, 2 * nd : 3 * nd] = dv[...].astype(BF)
        bias_sums[:, nd : 2 * nd] += eight_rows(grads_k)
        bias_sums[:, 2 * nd : 3 * nd] += eight_rows(dv[...])

        mean, spread = stats[group, 0:1], stats[group, 1:2]
        quarter = width // 4
        for part in range(4):
            cols = slice(part * quarter, (part + 1) * quarter)
            one = dot_nt(gg[group, 0:nq], w[cols, 0:nq])
            two = dot_nt(gg[group, nq:], w[cols, nq : nq + nf])
            scaled = (x[group, cols].astype(F32) - mean) * spread
            for slot, value in enumerate((one * scaled, one, two * scaled, two)):
                acc[slot, :, cols] += eight_rows(value)
            value = one * gains[0:1, cols] + two * gains[2:3, cols]
            store_shards(place, tz, (out_own, out_sib), g, cols, value)
    sums[...] = jnp.zeros_like(sums)
    own = cot[rows_at(place[1] * rows, rows), :].astype(F32)
    acc[4] = eight_rows(own)
    step = width // chips
    for i in range(5):
        total = jnp.sum(acc[i], axis=0, keepdims=True)
        if step % 128 == 0:
            for r in range(chips):
                at = pl.ds(pl.multiple_of((place[3] ^ r) * step, step), step)
                sums[i : i + 1, at] = total[:, r * step : (r + 1) * step]
        else:
            sums[i : i + 1, :] = total
    total = jnp.sum(bias_sums[...], axis=0, keepdims=True)
    sums[5:6, pl.ds(pl.multiple_of(place[0] * nq, nq), nq)] = by_head(total[:, :nq], heads)
    sums[6:7, pl.ds(pl.multiple_of(place[0] * nf, nf), nf)] = total[:, nq:]
    put_sums(out_sib, length, sums[...])


def put_sums(out, row, value):
    high = value.astype(BF).astype(F32)
    out[row : row + 16, :] = jnp.concatenate([high, value - high], axis=0).astype(BF)


def get_sums(ref, row):
    value = ref[row : row + 16, :].astype(F32)
    return value[0:8] + value[8:16]


def combine_body(tz, place, own, other, *outs):
    rows = own.shape[0] // tz
    for r, out in enumerate(outs):
        at = slice(r * rows, (r + 1) * rows)
        out[0:rows, :] = (own[at, :].astype(F32) + other[at, :].astype(F32)).astype(out.dtype)


def by_kind(values, heads):
    parts = [
        values[..., (h * 3 + kind) * HD : (h * 3 + kind + 1) * HD]
        for kind in range(3)
        for h in range(heads)
    ]
    return jnp.concatenate(parts, axis=-1)


def by_head(values, heads):
    parts = [
        values[..., (kind * heads + h) * HD : (kind * heads + h + 1) * HD]
        for h in range(heads)
        for kind in range(3)
    ]
    return jnp.concatenate(parts, axis=-1)


def pack_body(sizes, place, qkv_in, fc1_in, dense_in, fc2_in, kept, given, *scratch):
    nq, nf, nd = sizes
    qkv, fc1, dense, fc2, sems = scratch
    wait_all(
        start_all([(qkv_in, qkv), (fc1_in, fc1), (dense_in, dense), (fc2_in, fc2)], sems)
    )
    for out, which in ((given, 1 - place[0]), (kept, place[0])):

        def half(ref, size):
            return ref[:, pl.ds(pl.multiple_of(which * size, size), size)]

        out[:, 0:nq] = by_kind(half(qkv, nq), nd // HD)
        out[:, nq : nq + nf] = half(fc1, nf)
        out[:, nq + nf : nq + nf + nd] = half(dense, nd)
        out[:, nq + nf + nd :] = half(fc2, nf)


def split_body(tz, place, own, other, *refs):
    sums, outs = refs[: -tz - 1], refs[-tz - 1 :]
    combine_body(tz, place, own, other, *outs[:tz])
    add_sums(sums, outs[tz])


def add_sums(refs, out):
    total = refs[0][...]
    for one in refs[1:]:
        total = total + one[...]
    out[...] = total


def pass_body(place, shard, passed, out):
    rows = shard.shape[0]
    keep = (place[2] == 1).astype(F32)
    out[0:rows, :] = (shard[...].astype(F32) + keep * passed[...].astype(F32)).astype(BF)


def relay_body(place, near, shard, passed, *refs):
    first, second, sums = refs[:4], refs[4:8], refs[8:-5]
    out_near, out_shard, out_x, out_y, out_sums = refs[-5:]
    rows = near.shape[0]
    add_sums(sums, out_sums)
    total = out_sums[...]
    out_near[0:rows, :] = near[...]
    pass_body(place, shard, passed, out_shard)
    for out in (out_near, out_shard):
        put_sums(out, rows, total)
    at = 0
    for to_x, to_y, from_y, from_x in (first, second):
        size, columns = to_x.shape
        cols = slice(at, at + columns)
        out_x[:, cols] = to_x[...] + from_y[size : 2 * size, :]
        out_y[:, cols] = to_y[...] + from_x[size : 2 * size, :]
        at += columns


def other_body(place, first, first_x, second, second_x, from_y, out):
    size, at = out.shape[0], 0
    for mine, from_x in ((first, first_x), (second, second_x)):
        cols = slice(at, at + mine.shape[1])
        out[:, cols] = (
            mine[...].astype(F32) + from_x[0:size, :].astype(F32) + from_y[:, cols].astype(F32)
        ).astype(BF)
        at += mine.shape[1]


def finish_body(place, own, first, second, across, x, cot, sums, third, out_rows, out_sums):
    rows = own.shape[0]
    keep = (place[2] == 1).astype(F32)
    back = (
        own[...]
        + first[0:rows, :].astype(F32)
        + second[0:rows, :].astype(F32)
        + keep * across[...].astype(F32)
    )
    value = x[...].astype(F32)
    center = value - jnp.mean(value, axis=1, keepdims=True)
    spread = lax.rsqrt(jnp.mean(center * center, axis=1, keepdims=True) + EPS)
    scaled = center * spread
    out_rows[...] = cot[...].astype(F32) + spread * (
        back
        - jnp.mean(back, axis=1, keepdims=True)
        - scaled * jnp.mean(back * scaled, axis=1, keepdims=True)
    )
    out_sums[...] = sums[...] + get_sums(first, rows) + get_sums(second, rows) + third[...]


def join_body(heads, widths, count, place, *refs):
    parts, other, outs = refs[:count], refs[count], refs[count + 1 :]
    rows = other.shape[0]
    sums, at = [], 0
    while at < count:
        total, columns = parts[at][0:rows, :].astype(F32), parts[at].shape[1]
        at += 1
        while at < count and parts[at].shape[1] == columns:
            total = total + parts[at][0:rows, :].astype(F32)
            at += 1
        sums.append(total)
    if len(sums) == 3:
        sums = [jnp.concatenate(sums[:2], axis=1) + sums[2]]
    for half, which in ((sums[0], place[0]), (other[...].astype(F32), 1 - place[0])):
        at = 0
        for i, (out, size) in enumerate(zip(outs, widths)):
            value = half[:, at : at + size]
            if i == 0 and heads:
                value = by_head(value, heads)
            out[:, pl.ds(pl.multiple_of(which * size, size), size)] = value
            at += size


def xor_pairs(size, flip):
    return [(i, i ^ flip) for i in range(size)]


def on_device(
    dp,
    tz,
    inputs,
    segment_ids,
    ln1_gain,
    ln1_bias,
    ln2_gain,
    ln2_bias,
    qkv_weight,
    qkv_bias,
    dense_weight,
    dense_bias,
    fc1_weight,
    fc1_bias,
    fc2_weight,
    fc2_bias,
    cotangent,
):
    rows, width = inputs.shape
    length = segment_ids.shape[0]
    tokens = 2 * length
    chips = dp // 2
    here = lax.axis_index("dp")
    core = here % 2
    chip = here // 2
    tensor = lax.axis_index("tensor")
    step = width // chips
    nq, nf, nd = qkv_weight.shape[1] // 2, fc1_weight.shape[1] // 2, dense_weight.shape[1] // 2
    wide = nq + nf + nd + nf
    heads = nd // HD
    sizes = (length, width, nq, nf, nd)
    middle = (tensor == 1) | (tensor == 2)
    place = jnp.stack([core, tensor, middle, chip]).astype(jnp.int32)

    def turn(values):
        parts = [
            lax.dynamic_slice_in_dim(values, (chip ^ r) * step, step, axis=values.ndim - 1)
            for r in range(chips)
        ]
        return jnp.concatenate(parts, axis=-1)

    def sibling(values):
        return lax.ppermute(values, "dp", xor_pairs(dp, 1))

    def over_chip(values, flip):
        return lax.ppermute(values, "dp", xor_pairs(dp, 2 * flip))

    def over_tensor(values, flip):
        return lax.ppermute(values, "tensor", xor_pairs(tz, flip))

    def together(*values):
        return lax.optimization_barrier(values)

    def after(values, event):
        return lax.optimization_barrier((values, event))[0]

    def over_middle(values):
        return lax.ppermute(values, "tensor", [(0, 0), (1, 2), (2, 1), (3, 3)])

    def add_sibling(place, own, other):
        dtypes = [F32] + [BF] * (tz - 1)
        return kernel_call(
            partial(combine_body, tz),
            "add_sibling",
            [shape((rows, width), d) for d in dtypes],
            (place, own, other),
            [],
            LITTLE,
        )

    def added(parts):
        total = parts[0]
        for one in parts[1:]:
            total = total + one.astype(F32)
        return total

    def row_tables(arrived):
        both_ids = jnp.stack([segment_ids, sibling(after(segment_ids, arrived))])
        earlier = (both_ids[:, None, :] >= 0) & (both_ids[:, None, :] < both_ids[:, :, None])
        begins = jnp.sum(earlier.astype(jnp.int32), axis=2).reshape(tokens)
        flat_ids = both_ids.reshape(tokens)
        index = jnp.arange(tokens, dtype=jnp.int32) % length
        position = (index - begins).astype(F32)
        lane = jnp.arange(nd, dtype=jnp.int32) % HD
        half_rot = ROT // 2
        frequency = jnp.where(
            lane < ROT, 10000.0 ** (-2.0 * (lane % half_rot).astype(F32) / ROT), 0.0
        )
        angles = position[:, None] * frequency[None, :]
        sign = jnp.where(lane < half_rot, -1.0, 1.0)
        lower = jnp.where(flat_ids >= 0, begins, index).astype(F32)
        valid = (flat_ids >= 0).astype(F32)
        last = jnp.where(jnp.arange(128)[None, :] < 64, lower[:, None], valid[:, None])
        return jnp.concatenate([jnp.cos(angles), jnp.sin(angles) * sign, last], axis=1)

    def gather(kept, given, own_rows, later):
        if chips != 4 or tz != 4:
            blocks = [(kept, sibling(given))]
            flip = 1
            while flip < chips:
                blocks = blocks + [(over_chip(a, flip), over_chip(b, flip)) for a, b in blocks]
                flip *= 2
            shards = [own_rows] + [over_tensor(own_rows, r) for r in range(1, tz)]
            return (
                [one for block in blocks for one in block],
                shards + [sibling(one) for one in shards],
                later,
                row_tables(given),
            )
        moved = [over_tensor(own_rows, r) for r in range(1, tz)]
        kept_x, kept_y, given = together(over_chip(kept, 1), over_chip(kept, 2), sibling(given))
        table = row_tables(kept_x)
        given_x, given_y = over_chip(given, 1), over_chip(given, 2)
        moved, kept_x, given_x, given_y, table = together(moved, kept_x, given_x, given_y, table)
        later = after(later, moved)
        pieces = [kept, given, kept_x, given_x, kept_y, given_y]
        pieces += [over_chip(kept_x, 2), over_chip(given_y, 1)]
        shards = [own_rows] + moved
        return pieces, shards + [sibling(one) for one in shards], later, table

    rounds = chips == 4 and tz == 4
    packets = [[0], [1], [4, 6], [3, 7], [2], [5]] if rounds else [[i] for i in range(dp)]

    def first_round(parts):
        if rounds:
            return [over_chip(parts[2], 2), over_chip(parts[3], 1)]
        return []

    def chip_sums(parts):
        blocks = [(parts[2 * r], parts[2 * r + 1]) for r in range(chips)]
        flip = chips // 2
        while flip:
            blocks = [
                tuple(
                    (a.astype(F32) + over_chip(b, flip).astype(F32)).astype(BF)
                    for a, b in zip(blocks[r], blocks[r + flip])
                )
                for r in range(flip)
            ]
            flip //= 2
        return blocks[0]

    def join(terms, other, widths, own_heads):
        return kernel_call(
            partial(join_body, own_heads, widths, len(terms)),
            "join_halves",
            [shape((width // dp, 2 * one), F32) for one in widths],
            (place, *terms, other),
            [],
            LITTLE,
        )

    def half_of(values, which):
        size = values.shape[-1] // 2
        return lax.dynamic_slice_in_dim(values, which * size, size, axis=values.ndim - 1)


    kept, given = kernel_call(
        partial(pack_body, (nq, nf, nd)),
        "pack_weights",
        [shape((width // dp, wide), BF)] * 2,
        (place,),
        [
            pltpu.VMEM(one.shape, BF) for one in (qkv_weight, fc1_weight, dense_weight, fc2_weight)
        ]
        + [pltpu.SemaphoreType.DMA((4,))],
        LITTLE,
        [
            pltpu.with_memory_space_constraint(one, pltpu.HBM)
            for one in (qkv_weight, fc1_weight, dense_weight, fc2_weight)
        ],
    )

    own_rows = turn(after(inputs, kept))
    own_validity = lax.dynamic_slice_in_dim(segment_ids, tensor * rows, rows) >= 0
    masked = jnp.where(own_validity[:, None], turn(cotangent), jnp.zeros((), BF))
    weights, x_shards, masked, table = gather(kept, given, own_rows, masked)
    c_moved = [over_tensor(masked, r) for r in range(1, tz)]
    masked_sib = sibling(masked)

    gains = turn(jnp.stack([ln1_gain, ln1_bias, ln2_gain, ln2_bias]))
    shift_qkv = by_kind(half_of(qkv_bias, core), heads)[None, :]
    shift_fc1 = half_of(fc1_bias, core)[None, :]

    part_own, part_sib, x, w, n1, n2, qkv, lse, aa, dgelu, stats = kernel_call(
        partial(forward_body, tz, dp, len(weights), sizes),
        "forward",
        [
            shape((length, width), BF),
            shape((length, width), BF),
            shape((tokens, width), BF),
            shape((width, wide), BF),
            shape((tokens, width), BF),
            shape((tokens, width), BF),
            shape((tokens, nq), BF),
            shape((tokens, 128), F32),
            shape((tokens, nd + nf), BF),
            shape((tokens, nf), BF),
            shape((tokens, 128), F32),
        ],
        (after(place, masked_sib), table, gains, shift_qkv, shift_fc1),
        [pltpu.SemaphoreType.DMA((2 * tz,)), pltpu.SemaphoreType.DMA((dp,))],
        LITTLE,
        (*x_shards, *weights),
    )

    c_moved, part_sib = together(c_moved, part_sib)
    part_other = sibling(part_sib)
    branch_shards = add_sibling(place, part_own, part_other)
    c_shards = [masked] + c_moved + [masked_sib]
    c_shards += [sibling(one) for one in after(c_moved, part_other)]
    if rounds:
        passed, across = over_tensor(branch_shards[3], 1), over_middle(branch_shards[3])
    cot, *second_parts = kernel_call(
        partial(second_grads_body, tz, dp, packets),
        "second_grads",
        [shape((tokens, width), BF)]
        + [shape((width // dp * len(packet), nd + nf), BF) for packet in packets],
        (after(place, branch_shards[1]), aa),
        [pltpu.SemaphoreType.DMA((2 * tz,))],
        LITTLE,
        c_shards,
    )

    if rounds:
        shard = kernel_call(
            pass_body,
            "branch_relay",
            [shape((rows, width), BF)],
            (after(place, second_parts[0]), branch_shards[2], passed),
            [],
            LITTLE,
        )[0]
        branch_moved = [over_tensor(branch_shards[1], 1), over_tensor(shard, 2)]
        branch_moved += [across]
    else:
        shard = branch_shards[1]
        branch_moved = [over_tensor(branch_shards[r], r) for r in range(1, tz)]
    second_first = first_round(second_parts)
    back_own, back_sib, gg, sums = kernel_call(
        partial(backward_body, tz, chips, sizes),
        "backward",
        [
            shape((length, width), BF),
            shape((length + 16, width), BF),
            shape((tokens, nq + nf), BF),
            shape((8, width), F32),
        ],
        (
            after(place, shard),
            table,
            gains,
            cot,
            w,
            qkv,
            lse,
            dgelu,
            stats,
            x,
        ),
        [
            pltpu.VMEM((5, 8, width), F32),
            pltpu.VMEM((length, nd), F32),
            pltpu.VMEM((length, nd), F32),
            pltpu.VMEM((8, nq + nf), F32),
        ],
        14,
    )
    first_parts = kernel_call(
        partial(first_grads_body, dp, packets, nq),
        "first_grads",
        [shape((width // dp * len(packet), nq + nf), BF) for packet in packets],
        (place, n1, n2, gg),
        [],
        LITTLE,
    )
    branch_moved, second_first, back_sib = together(
        branch_moved, second_first, after(back_sib, first_parts[0])
    )
    if rounds:
        branch_moved[2] = jnp.where(middle, branch_moved[2], jnp.zeros((), BF))
    output = (
        inputs.astype(F32)
        + turn(added([branch_shards[0]] + branch_moved))
        + dense_bias
        + fc2_bias
    ).astype(BF)

    if rounds:
        back_other = sibling(back_sib)
        first_parts = list(first_parts)
        sums_chips = [over_chip(sums, flip) for flip in range(1, chips)]
        first_parts[2], first_parts[3], sums_chips = together(
            first_parts[2], first_parts[3], sums_chips
        )
        first_first = first_round(first_parts)
        *back_shards, sums = kernel_call(
            partial(split_body, tz),
            "split_back",
            [shape((rows, width), F32)]
            + [shape((rows, width), BF)] * 3
            + [shape(sums.shape, F32)],
            (place, back_own, back_other, sums, *sums_chips),
            [],
            LITTLE,
        )
        passed, across = over_tensor(back_shards[3], 1), over_middle(back_shards[3])
        near, shard, from_x, from_y, sums = kernel_call(
            relay_body,
            "second_round",
            [
                shape((rows + 16, width), BF),
                shape((rows + 16, width), BF),
                shape((width // dp, wide), BF),
                shape((width // dp, wide), BF),
                shape(sums.shape, F32),
            ],
            (
                after(place, across),
                back_shards[1],
                back_shards[2],
                passed,
                first_parts[4],
                first_parts[5],
                *first_first,
                second_parts[4],
                second_parts[5],
                *second_first,
                sums,
                sibling(sums),
            ),
            [],
            LITTLE,
        )
        biases = sums
        back_second, back_first = over_tensor(shard, 2), over_tensor(near, 1)
        third = over_tensor(sums, 3)
        from_x, from_y = over_chip(from_x, 1), over_chip(from_y, 2)
        other = kernel_call(
            other_body,
            "other_sums",
            [shape((width // dp, wide), BF)],
            (place, first_parts[1], first_first[1], second_parts[1], second_first[1], from_y),
            [],
            LITTLE,
        )[0]
        own_parts = [first_parts[0], first_first[0], second_parts[0], second_first[0], from_x]
        qkv_grad, fc1_grad, dense_grad, fc2_grad = join(
            own_parts, sibling(other), (nq, nf, nd, nf), heads
        )
        input_grad, sums = kernel_call(
            finish_body,
            "finish_rows",
            [shape((rows, width), F32), shape(sums.shape, F32)],
            (
                after(place, other),
                back_shards[0],
                back_first,
                back_second,
                across,
                own_rows,
                masked,
                sums,
                third,
            ),
            [],
            6,
        )
    else:
        back_other = sibling(back_sib)
        back_shards = add_sibling(place, back_own, back_other)
        back = added([back_shards[0]] + [over_tensor(back_shards[r], r) for r in range(1, tz)])
        sums = added([sums, back_other[length : length + 8], back_other[length + 8 :]])
        if step % 128:
            sums = jnp.concatenate([turn(sums[:5]), sums[5:]], axis=0)
        value = own_rows.astype(F32)
        center = value - jnp.mean(value, axis=1, keepdims=True)
        spread = lax.rsqrt(jnp.mean(center * center, axis=1, keepdims=True) + EPS)
        scaled = center * spread
        input_grad = masked.astype(F32) + spread * (
            back
            - jnp.mean(back, axis=1, keepdims=True)
            - scaled * jnp.mean(back * scaled, axis=1, keepdims=True)
        )
        (second_own, second_other), (first_own, first_other) = (
            chip_sums(second_parts),
            chip_sums(first_parts),
        )
        second_sib, first_sib = sibling(second_other), sibling(first_other)
        flip = 1
        while flip < chips:
            sums = sums + over_chip(sums, flip)
            flip *= 2
        biases = sums
        sums = added([sums] + [over_tensor(sums, r) for r in range(1, tz)])
        dense_grad, fc2_grad = join([second_own], second_sib, (nd, nf), 0)
        qkv_grad, fc1_grad = join([first_own], first_sib, (nq, nf), heads)
    input_grad = turn(input_grad)

    return (
        output,
        input_grad,
        sums[0],
        sums[1],
        sums[2],
        sums[3],
        qkv_grad,
        biases[5, : 2 * nq],
        dense_grad,
        sums[4],
        fc1_grad,
        biases[6, : 2 * nf],
        fc2_grad,
        sums[4],
    )


def solution(mesh):
    return jax.shard_map(
        partial(on_device, mesh.shape["dp"], mesh.shape["tensor"]),
        mesh=mesh,
        in_specs=(
            P(("dp", "tensor"), None),
            P("dp"),
            P(),
            P(),
            P(),
            P(),
            P("dp", "tensor"),
            P("tensor"),
            P("dp", "tensor"),
            P(),
            P("dp", "tensor"),
            P("tensor"),
            P("dp", "tensor"),
            P(),
            P(("dp", "tensor"), None),
        ),
        out_specs=(
            P(("dp", "tensor"), None),
            P(("dp", "tensor"), None),
            P(),
            P(),
            P(),
            P(),
            P("dp", "tensor"),
            P("tensor"),
            P("dp", "tensor"),
            P(),
            P("dp", "tensor"),
            P("tensor"),
            P("dp", "tensor"),
            P(),
        ),
        check_vma=False,
    )
```
